512 devices in a mesh: bucket: 16 (over z, core), ref: 32 (over x, y).
Axes of the slice: x: 4, y: 8, z: 8, core: 2. Of those that a mesh axis runs over, the one named last changes fastest.
Arguments:
- gen_points: bfloat16 [68, 49152], P(None, 'bucket'), may hold values from -6 to 6
- bucket_id: int32 [49152], P('bucket'), may hold values from 0 to 15, as said below
- ref_points: bfloat16 [16384, 68, 128], P(('bucket', 'ref')), may hold values from -6 to 6
- block_pairs: int32 [16, 32, 2, 768], P('bucket', 'ref'), may hold values from 0 to 31, as said below
- pair_count: int32 [16, 32], P('bucket', 'ref'), may hold values from 32 to 768, as said below
Outputs:
- gen_dist: float32 [49152], P('bucket')
- ref_dist: float32 [16384, 128], P(('bucket', 'ref'))
The draws below stay inside these ranges and needn't reach their ends.
Inputs may be any that keep to these rules, and one draw needn't show every extreme that they name: `bucket_id`: every source sends between 129 and 256 of its 3072 points to every bucket; in every draw some bucket receives exactly 256 points from every source. `block_pairs`: row 0 holds numbers below 32, row 1 numbers below 32. Among the live pairs of a device every one of its reference blocks is named, and every generated block of a bucket is named by a live pair on some shard of that bucket. `pair_count`: some device's list is full in every draw.
All inputs are finite; a program needn't handle non-finite values.
Results may differ from the reference program's by a relative error of at most 0.0003.
Values may be sent and summed in bfloat16 or wider, within the bound.
A program may use at most 64 MiB of HBM per device.

```python
import jax
import jax.numpy as jnp
from jax import lax

F = 68
BLK = 128
RBLK = 32
OWNERS = 16
SHARDS = 32
CAP = 256
GEN_DEV = 3072
PAIRS = 768
NG = 49152
REF_BLOCKS = 16384


def source_buckets(key, full_bucket):
    key_slots, key_order = jax.random.split(key)
    others = OWNERS - 1
    room = CAP - BLK - 1
    extra = GEN_DEV - CAP - others * (BLK + 1)
    slot_owner = jnp.repeat(jnp.arange(others, dtype=jnp.int32), room)
    chosen = jax.random.permutation(key_slots, slot_owner)[:extra]
    added = jnp.sum((chosen[None, :] == jnp.arange(others, dtype=jnp.int32)[:, None]).astype(jnp.int32), axis=1)
    virtual = jnp.concatenate([jnp.full((1,), CAP, jnp.int32), BLK + 1 + added])
    counts = virtual[(jnp.arange(OWNERS, dtype=jnp.int32) - full_bucket) % OWNERS]
    bounds = jnp.cumsum(counts)
    position = jnp.arange(GEN_DEV, dtype=jnp.int32)
    ordered = jnp.sum((position[:, None] >= bounds[None, :]).astype(jnp.int32), axis=1)
    return ordered[jax.random.permutation(key_order, GEN_DEV)]


def draw_bucket_id(key, part):
    full_bucket = jax.random.randint(jax.random.fold_in(key, 7), (), 0, OWNERS)

    def one_source(index):
        return source_buckets(jax.random.fold_in(key, 100 + index), full_bucket)
    return jax.vmap(one_source)(jnp.arange(OWNERS, dtype=jnp.int32)).reshape(NG).astype(jnp.int32)


def draw_block_pairs(key, part):

    def one_device(index):
        owner = index // SHARDS
        shard = index % SHARDS
        shift = jax.random.randint(jax.random.fold_in(key, 17 + owner), (), 0, 2 * OWNERS)
        key_perm, key_gen, key_ref = jax.random.split(jax.random.fold_in(key, 5000 + index), 3)
        cover_ref = jax.random.permutation(key_perm, RBLK).astype(jnp.int32)
        cover_gen = (jnp.arange(RBLK, dtype=jnp.int32) + shard * RBLK + shift) % (2 * OWNERS)
        rest_gen = jax.random.randint(key_gen, (PAIRS - RBLK,), 0, 2 * OWNERS)
        rest_ref = jax.random.randint(key_ref, (PAIRS - RBLK,), 0, RBLK)
        return jnp.stack([jnp.concatenate([cover_gen, rest_gen]), jnp.concatenate([cover_ref, rest_ref])]).astype(jnp.int32)
    lists = jax.vmap(one_device)(jnp.arange(OWNERS * SHARDS, dtype=jnp.int32))
    return lists.reshape(OWNERS, SHARDS, 2, PAIRS)


def draw_pair_count(key, part):
    key_first, key_second, key_full = jax.random.split(jax.random.fold_in(key, 3), 3)
    spread = PAIRS - RBLK
    first = jax.random.randint(key_first, (OWNERS * SHARDS,), 0, spread + 1)
    second = jax.random.randint(key_second, (OWNERS * SHARDS,), 0, spread + 1)
    counts = RBLK + first * second // spread
    busiest = jax.random.randint(key_full, (), 0, OWNERS * SHARDS)
    flat = jnp.where(jnp.arange(OWNERS * SHARDS, dtype=jnp.int32) == busiest, PAIRS, counts)
    return flat.reshape(OWNERS, SHARDS).astype(jnp.int32)


def level_of(stream_key, extent, cuts, smallest, largest):
    def one(dim, shards_of):
        draws = jax.random.uniform(jax.random.fold_in(jax.random.fold_in(stream_key, 6), dim), (shards_of,), jnp.float32, smallest / len(cuts), largest / len(cuts))
        return jnp.repeat(jnp.exp(draws), extent[dim] // shards_of).reshape((-1,) + (1,) * (len(extent) - dim - 1))

    factor_of = one(*cuts[0])
    for cut in cuts[1:]:
        factor_of = factor_of * one(*cut)
    return factor_of


def scatter_about(stream_key, dims, scale, bound, pieces=(), kind=jnp.bfloat16):
    values = scale * jax.random.normal(stream_key, dims, jnp.float32)
    if pieces:
        values = values * level_of(stream_key, dims, pieces, -0.22, 0.18)
    return jnp.clip(values, -bound, bound).astype(kind)


def setup_inputs(seed: int = 0) -> dict:
    seeds = jax.random.split(jax.random.key(seed), 6)
    return {
        "gen_points": scatter_about(seeds[0], (F, NG), 1.0, 6.0, ((1, 16),)),
        "bucket_id": draw_bucket_id(jax.random.fold_in(seeds[5], 71), 0),
        "ref_points": scatter_about(seeds[2], (REF_BLOCKS, F, BLK), 1.0, 6.0, ((0, 512),)),
        "block_pairs": draw_block_pairs(jax.random.fold_in(seeds[5], 71), 0),
        "pair_count": draw_pair_count(jax.random.fold_in(seeds[5], 71), 0),
    }


def tile_minima(gen_blocks, gen_norm, gen_live, ref_blocks, ref_norm, pair_list, live_count):
    pair_total = PAIRS
    step_len = 64
    while pair_total % step_len != 0:
        step_len = step_len // 2
    gen_count = gen_blocks.shape[0]
    ref_count = ref_blocks.shape[0]
    gen_ids = jnp.arange(gen_count, dtype=jnp.int32)
    ref_ids = jnp.arange(ref_count, dtype=jnp.int32)

    def advance(state_pair, offset):
        row_min, col_min = state_pair
        gen_pick = lax.dynamic_slice_in_dim(pair_list[0], offset, step_len)
        ref_pick = lax.dynamic_slice_in_dim(pair_list[1], offset, step_len)
        active = (offset + jnp.arange(step_len, dtype=jnp.int32)) < live_count
        gen_tiles = gen_blocks[gen_pick].astype(jnp.float32)
        ref_tiles = ref_blocks[ref_pick].astype(jnp.float32)
        products = jnp.einsum("pfi,pfj->pij", gen_tiles, ref_tiles, precision=lax.Precision.HIGHEST)
        distance = (gen_norm[gen_pick][:, :, None] + ref_norm[ref_pick][:, None, :] - 2.0 * products) / F
        row_part = jnp.min(jnp.where(active[:, None, None], distance, jnp.inf), axis=2)
        col_ok = active[:, None, None] & (gen_live[gen_pick][:, :, None] > 0)
        col_part = jnp.min(jnp.where(col_ok, distance, jnp.inf), axis=1)
        row_hit = gen_pick[None, :] == gen_ids[:, None]
        row_min = jnp.minimum(row_min, jnp.min(jnp.where(row_hit[:, :, None], row_part[None], jnp.inf), axis=1))
        col_hit = ref_pick[None, :] == ref_ids[:, None]
        col_min = jnp.minimum(col_min, jnp.min(jnp.where(col_hit[:, :, None], col_part[None], jnp.inf), axis=1))
        return (row_min, col_min), None

    offsets = jnp.arange(0, pair_total, step_len, dtype=jnp.int32)
    initial = (jnp.full((gen_count, BLK), jnp.inf, jnp.float32), jnp.full((ref_count, BLK), jnp.inf, jnp.float32))
    (row_min, col_min), ignored = lax.scan(advance, initial, offsets)
    return row_min, col_min


def reference(gen_points, bucket_id, ref_points, block_pairs, pair_count):
    source_ids = bucket_id.reshape(OWNERS, GEN_DEV)
    owner_ids = jnp.arange(OWNERS, dtype=jnp.int32)
    matches = (source_ids[:, None, :] == owner_ids[None, :, None]).astype(jnp.int32)
    earlier = jnp.cumsum(matches, axis=2) - matches
    slot_rank = jnp.sum(earlier * matches, axis=1)
    sources = jnp.arange(OWNERS, dtype=jnp.int32)[:, None]
    block_index = 2 * sources + slot_rank // BLK
    slot_offset = slot_rank % BLK
    points = jnp.transpose(gen_points.reshape(F, OWNERS, GEN_DEV), (1, 2, 0))
    arranged = jnp.zeros((OWNERS, 2 * OWNERS, F, BLK), jnp.bfloat16).at[source_ids, block_index, :, slot_offset].set(points)
    live_cols = jnp.zeros((OWNERS, 2 * OWNERS, BLK), jnp.int32).at[source_ids, block_index, slot_offset].set(1)
    arranged_f = arranged.astype(jnp.float32)
    gen_norms = jnp.sum(arranged_f * arranged_f, axis=2)
    ref_f = ref_points.astype(jnp.float32)
    ref_norms = jnp.sum(ref_f * ref_f, axis=1)

    def per_device(index):
        owner = index // SHARDS
        shard = index % SHARDS
        ref_blocks = lax.dynamic_slice_in_dim(ref_points, (index * RBLK).astype(jnp.int32), RBLK, 0)
        ref_norm = lax.dynamic_slice_in_dim(ref_norms, (index * RBLK).astype(jnp.int32), RBLK, 0)
        return tile_minima(arranged[owner], gen_norms[owner], live_cols[owner], ref_blocks, ref_norm, block_pairs[owner, shard], pair_count[owner, shard])

    rows_all, cols_all = lax.map(per_device, jnp.arange(OWNERS * SHARDS, dtype=jnp.int32))
    row_min = jnp.min(rows_all.reshape(OWNERS, SHARDS, 2 * OWNERS, BLK), axis=1)
    gen_dist = row_min[source_ids, block_index, slot_offset].reshape(NG)
    ref_dist = cols_all.reshape(REF_BLOCKS, BLK)
    return gen_dist, ref_dist
```

```python
import jax
import jax.numpy as jnp
from jax import lax
from jax.experimental import pallas as pl
from jax.experimental.pallas import tpu as pltpu
from jax.sharding import PartitionSpec as P

F = 68
BLK = 128
NB = 16
NR = 32
NX = 4
NY = 8
GEN = 3072
Q = GEN // BLK
PAIRS = 768
SEND = 80
K = 128
TJ = 256
BIG = 1e30
MESH = pl.DeviceIdType.MESH
bf16 = jnp.bfloat16
f32 = jnp.float32


def iota(shape, dim):
    return lax.broadcasted_iota(jnp.int32, shape, dim)


def three(v):
    hi = v.astype(bf16).astype(f32)
    mid = (v - hi).astype(bf16).astype(f32)
    lo = (v - hi - mid).astype(bf16).astype(f32)
    return hi, mid, lo


def kernel(
    gen_ref, bid_ref, rp_ref, pairs_ref, count_ref,
    gd_ref, rd_ref,
    onehot, rank_row, blk_row, ebuf, tmp, xbuf, mrow, rft, gsend, gbuf, gop, colacc,
    rows, red, fin, back, back2,
    s1_send, s1_recv, ring_send, ring_recv, a_send, a_recv, b_send, b_recv,
):
    b = lax.axis_index("bucket")
    r = lax.axis_index("ref")
    x, y = r // NY, lax.rem(r, NY)
    to_b, half = r // 2, lax.rem(r, 2)
    same = to_b == b
    sames = same.astype(jnp.int32)

    bar = pltpu.get_barrier_semaphore()

    def greet(i, c):
        pl.semaphore_signal(bar, inc=1, device_id=(b, lax.rem(r + i, NR)), device_id_type=MESH)
        return c

    lax.fori_loop(1, NR, greet, 0)

    def greet_source(i, c):
        db, dr = i // 2, 2 * b + lax.rem(i, 2)

        @pl.when(jnp.logical_not((db == b) & (dr == r)))
        def _():
            pl.semaphore_signal(bar, inc=1, device_id=(db, dr), device_id_type=MESH)

        return c

    lax.fori_loop(0, NR, greet_source, 0)

    for q in range(Q):
        ebuf[q * NB:(q + 1) * NB, :] = (bid_ref[q:q + 1, :] == iota((NB, BLK), 0)).astype(f32).astype(bf16)
    i0, i1 = iota((BLK, 2 * BLK), 0), iota((BLK, 2 * BLK), 1)
    tri = ((i0 < i1) | (i1 >= BLK)).astype(f32).astype(bf16)
    sums = jnp.dot(ebuf[...], tri, preferred_element_type=f32)
    carry = jnp.zeros((NB, BLK), f32)
    for q in range(Q):
        e = ebuf[q * NB:(q + 1) * NB, :].astype(f32)
        part = sums[q * NB:(q + 1) * NB, :]
        rank = jnp.sum(e * (part[:, :BLK] + carry), axis=0, keepdims=True)
        carry = carry + part[:, BLK:]
        over = rank >= BLK
        off = jnp.where(over, rank - BLK, rank)
        rank_row[:, q * BLK:(q + 1) * BLK] = off
        blk = 2 * bid_ref[q:q + 1, :] + over.astype(jnp.int32)
        blk_row[:, q * BLK:(q + 1) * BLK] = blk
        onehot[:, q * BLK:(q + 1) * BLK] = (iota((BLK, BLK), 0) == off.astype(jnp.int32)).astype(f32).astype(bf16)

    mine = (blk_row[...] == r).astype(f32)
    picked = (gen_ref[...].astype(f32) * mine).astype(bf16)
    block = lax.dot_general(picked, onehot[...], (((1,), (1,)), ((), ())), preferred_element_type=f32)
    norm = jnp.sum(block * block, axis=0, keepdims=True)
    total = jnp.sum(jnp.where(iota((NB, BLK), 0) == to_b, carry, 0.0), axis=0, keepdims=True)
    slot_id = iota((1, BLK), 1) + half * BLK
    norm = jnp.where(slot_id.astype(f32) < total, norm, BIG)
    hi, mid, lo = three(norm)
    tmp[F:SEND, :] = jnp.zeros((SEND - F, BLK), f32)
    tmp[0:F, :] = block
    tmp[F:F + 1, :] = hi
    tmp[F + 1:F + 2, :] = mid
    tmp[F + 2:F + 3, :] = lo
    tmp[F + 3:F + 6, :] = jnp.ones((3, BLK), f32)
    gsend[...] = tmp[...].astype(bf16)

    pl.semaphore_wait(bar, 2 * NR - 1 - sames)

    t = 2 * b + half
    tx, ty = t // NY, lax.rem(t, NY)
    t_slot = ty * NX + tx

    def first(i):
        return pltpu.make_async_remote_copy(
            src_ref=gsend, dst_ref=gbuf.at[t_slot],
            send_sem=s1_send.at[i], recv_sem=s1_recv.at[tx],
            device_id=(to_b, i * NY + ty), device_id_type=MESH,
        )

    for i in range(NX):
        here = same & (x == i)

        @pl.when(jnp.logical_not(here))
        def _():
            first(i).start()

        @pl.when(here)
        def _():
            gbuf[t_slot] = gsend[...]

    kid = iota((K, PAIRS), 0) - SEND
    gid = jnp.where((kid >= 0) & (kid < NR), lax.rem(kid, NX) * NY + kid // NX, -1)
    live = iota((1, PAIRS), 1) < count_ref[0, 0]
    named = jnp.where(live, pairs_ref[0, 0, 0:1, :], -2)
    a_hot = (gid == named).astype(f32).astype(bf16)
    b_hot = (iota((NR, PAIRS), 0) == pairs_ref[0, 0, 1:2, :]).astype(f32).astype(bf16)
    listed = lax.dot_general(b_hot, a_hot, (((1,), (1,)), ((), ())), preferred_element_type=f32)
    lane = iota((NR, K), 1)
    mrow[...] = jnp.where(
        (lane >= SEND) & (lane < SEND + NR) & (listed < 0.5), BIG,
        jnp.where((lane >= F) & (lane < F + 3), 1.0, 0.0),
    )

    xbuf[F:K, :] = jnp.zeros((K - F, BLK), f32)

    def prepare(k, c):
        v = rp_ref[k].astype(f32)
        rh, rm, rl = three(jnp.sum(v * v, axis=0, keepdims=True))
        xbuf[0:F, :] = -2.0 * v
        xbuf[F + 3:F + 4, :] = rh
        xbuf[F + 4:F + 5, :] = rm
        xbuf[F + 5:F + 6, :] = rl
        at = pl.multiple_of(k * BLK, BLK)
        rft[pl.ds(at, BLK), :] = (xbuf[...].T + mrow[pl.ds(k, 1), :]).astype(bf16)
        return c

    lax.fori_loop(0, NR, prepare, 0)

    def settle(i, slot):
        g = lax.rem(slot, NX) * NY + slot // NX
        return pltpu.make_async_remote_copy(
            src_ref=rows.at[slot], dst_ref=red.at[r],
            send_sem=a_send, recv_sem=a_recv,
            device_id=(b, g), device_id_type=MESH,
        )

    def compute(group, is_first):
        for i in range(NX):
            slot = group * NX + i
            hot = (iota((K - SEND, BLK), 0) == slot).astype(f32).astype(bf16)
            gop[0:SEND, i * BLK:(i + 1) * BLK] = gbuf[slot]
            gop[SEND:K, i * BLK:(i + 1) * BLK] = hot

        def tile(j, acc):
            at = pl.multiple_of(j * TJ, TJ)
            d = jnp.dot(rft[pl.ds(at, TJ), :], gop[...], preferred_element_type=f32)
            acc = jnp.minimum(acc, jnp.min(d.reshape(TJ // 8, 8, NX * BLK), axis=0))
            m = jnp.minimum(
                jnp.minimum(d[:, 0:BLK], d[:, BLK:2 * BLK]),
                jnp.minimum(d[:, 2 * BLK:3 * BLK], d[:, 3 * BLK:4 * BLK]),
            )
            if not is_first:
                m = jnp.minimum(m, colacc[pl.ds(at, TJ), :])
            colacc[pl.ds(at, TJ), :] = m
            return acc

        acc = lax.fori_loop(0, NR * BLK // TJ, tile, jnp.full((8, NX * BLK), BIG, f32))
        low = jnp.min(acc, axis=0, keepdims=True)
        for i in range(NX):
            slot = group * NX + i
            rows[slot] = low[:, i * BLK:(i + 1) * BLK]
        for i in range(NX):
            slot = group * NX + i
            own = (group == y) & (x == i)

            @pl.when(jnp.logical_not(own))
            def _():
                settle(i, slot).start()

            @pl.when(own)
            def _():
                red[r] = rows[slot]

    for i in range(NX):
        src_b = (i * NY + y) // 2
        here = same & (x == i)

        @pl.when(jnp.logical_not(here))
        def _():
            first(i).wait_send()
            pltpu.make_async_remote_copy(
                src_ref=gsend, dst_ref=gbuf.at[y * NX + i],
                send_sem=s1_send.at[i], recv_sem=s1_recv.at[i],
                device_id=(src_b, r), device_id_type=MESH,
            ).wait_recv()

    def hop(way, step):
        sign = 1 if way == 0 else -1
        group = lax.rem(y - sign * (step - 1) + 2 * NY, NY)
        if step < NY // 2:
            piece = gbuf.at[pl.ds(group * NX, NX)]
        else:
            piece = gbuf.at[pl.ds(group * NX + way * (NX // 2), NX // 2)]
        to = lax.rem(y + sign + NY, NY)
        return pltpu.make_async_remote_copy(
            src_ref=piece, dst_ref=piece,
            send_sem=ring_send.at[way, step - 1], recv_sem=ring_recv.at[way, step - 1],
            device_id=(b, x * NY + to), device_id_type=MESH,
        )

    def arrival(way, step):
        sign = 1 if way == 0 else -1
        group = lax.rem(y - sign * step + 2 * NY, NY)
        if step < NY // 2:
            piece = gbuf.at[pl.ds(group * NX, NX)]
        else:
            piece = gbuf.at[pl.ds(group * NX + way * (NX // 2), NX // 2)]
        return pltpu.make_async_remote_copy(
            src_ref=piece, dst_ref=piece,
            send_sem=ring_send.at[way, step - 1], recv_sem=ring_recv.at[way, step - 1],
            device_id=(b, x * NY + lax.rem(y - sign + NY, NY)), device_id_type=MESH,
        )

    for way in range(2):
        hop(way, 1).start()
    compute(y, True)
    for step in range(1, NY // 2):
        for way in range(2):
            arrival(way, step).wait_recv()
            hop(way, step + 1).start()
        compute(lax.rem(y - step + NY, NY), False)
        compute(lax.rem(y + step, NY), False)
    for way in range(2):
        arrival(way, NY // 2).wait_recv()
    compute(lax.rem(y + NY // 2, NY), False)

    def finish(k, c):
        at = pl.multiple_of(k * BLK, BLK)
        v = colacc[pl.ds(at, BLK), :].T
        rd_ref[pl.ds(k, 1), :] = jnp.min(v, axis=0, keepdims=True) / F
        return c

    lax.fori_loop(0, NR, finish, 0)

    pltpu.make_async_copy(red.at[pl.ds(0, NR - 1)], red.at[pl.ds(0, NR - 1)], a_recv).wait()
    low = red[0]
    for i in range(1, NR):
        low = jnp.minimum(low, red[i])
    fin[0] = low / F

    def deliver(i, c):
        @pl.when(jnp.logical_not(same & (i == r)))
        def _():
            pltpu.make_async_remote_copy(
                src_ref=fin.at[0], dst_ref=back.at[t],
                send_sem=b_send, recv_sem=b_recv,
                device_id=(to_b, i), device_id_type=MESH,
            ).start()

        return c

    lax.fori_loop(0, NR, deliver, 0)

    @pl.when(same)
    def _():
        back[t] = fin[0]
        pltpu.make_async_copy(back.at[pl.ds(0, NR - 1)], back.at[pl.ds(0, NR - 1)], b_recv).wait()

    @pl.when(jnp.logical_not(same))
    def _():
        pltpu.make_async_copy(back.at[pl.ds(0, NR)], back.at[pl.ds(0, NR)], b_recv).wait()

    for i in range(NR):
        back2[i:i + 1, :] = back[i]
    hi, mid, lo = three(back2[...])
    parts = jnp.concatenate([hi, mid, lo], axis=0).astype(bf16)
    for q in range(0, Q, 4):
        cols = slice(q * BLK, (q + 4) * BLK)
        v = jnp.dot(parts, onehot[:, cols], preferred_element_type=f32)
        v = v[0:NR] + v[NR:2 * NR] + v[2 * NR:3 * NR]
        pick = iota((NR, 4 * BLK), 0) == blk_row[:, cols]
        v = jnp.sum(jnp.where(pick, v, 0.0), axis=0, keepdims=True)
        for i in range(4):
            gd_ref[q + i:q + i + 1, :] = v[:, i * BLK:(i + 1) * BLK]

    for way in range(2):
        for step in range(1, NY // 2 + 1):
            hop(way, step).wait_send()
    pltpu.make_async_copy(rows.at[pl.ds(0, NR - 1)], rows.at[pl.ds(0, NR - 1)], a_send).wait()

    @pl.when(same)
    def _():
        pltpu.make_async_copy(back.at[pl.ds(0, NR - 1)], back.at[pl.ds(0, NR - 1)], b_send).wait()

    @pl.when(jnp.logical_not(same))
    def _():
        pltpu.make_async_copy(back.at[pl.ds(0, NR)], back.at[pl.ds(0, NR)], b_send).wait()


def per_device(gen_points, bucket_id, ref_points, block_pairs, pair_count):
    vmem = pl.BlockSpec(memory_space=pltpu.VMEM)
    dma = pltpu.SemaphoreType.DMA
    gd, rd = pl.pallas_call(
        kernel,
        out_shape=(
            jax.ShapeDtypeStruct((Q, BLK), f32),
            jax.ShapeDtypeStruct((NR, BLK), f32),
        ),
        in_specs=[vmem] * 4 + [pl.BlockSpec(memory_space=pltpu.SMEM)],
        out_specs=(vmem, vmem),
        scratch_shapes=[
            pltpu.VMEM((BLK, GEN), bf16),
            pltpu.VMEM((1, GEN), f32),
            pltpu.VMEM((1, GEN), jnp.int32),
            pltpu.VMEM((Q * NB, BLK), bf16),
            pltpu.VMEM((SEND, BLK), f32),
            pltpu.VMEM((K, BLK), f32),
            pltpu.VMEM((NR, K), f32),
            pltpu.VMEM((NR * BLK, K), bf16),
            pltpu.VMEM((SEND, BLK), bf16),
            pltpu.VMEM((NR, SEND, BLK), bf16),
            pltpu.VMEM((K, NX * BLK), bf16),
            pltpu.VMEM((NR * BLK, BLK), f32),
            pltpu.VMEM((NR, 1, BLK), f32),
            pltpu.VMEM((NR, 1, BLK), f32),
            pltpu.VMEM((1, 1, BLK), f32),
            pltpu.VMEM((NR, 1, BLK), f32),
            pltpu.VMEM((NR, BLK), f32),
            dma((NX,)), dma((NX,)), dma((2, NY // 2)), dma((2, NY // 2)),
            dma, dma, dma, dma,
        ],
        compiler_params=pltpu.CompilerParams(
            collective_id=0, has_side_effects=True, vmem_limit_bytes=48 * 2**20
        ),
        cost_estimate=pl.CostEstimate(
            flops=2 * 4096 * 4096 * 128, bytes_accessed=2**21, transcendentals=0
        ),
        name="chamfer",
    )(gen_points, bucket_id.reshape(Q, BLK), ref_points, block_pairs, pair_count)
    return gd.reshape(GEN), rd


def solution(mesh):
    return jax.shard_map(
        per_device,
        mesh=mesh,
        in_specs=(
            P(None, "bucket"),
            P("bucket"),
            P(("bucket", "ref"), None, None),
            P("bucket", "ref", None, None),
            P("bucket", "ref"),
        ),
        out_specs=(P("bucket"), P(("bucket", "ref"), None)),
        check_vma=False,
    )
```

```python
import jax
import jax.numpy as jnp
from jax import lax
from jax.experimental import pallas as pl
from jax.experimental.pallas import tpu as pltpu
from jax.sharding import PartitionSpec as P

F = 68
BLK = 128
NB = 16
NR = 32
NX = 4
NY = 8
GEN = 3072
Q = GEN // BLK
PAIRS = 768
SEND = 80
K = 128
UN = 8
BIG = 1e30
MESH = pl.DeviceIdType.MESH
bf16 = jnp.bfloat16
f32 = jnp.float32


def iota(shape, dim):
    return lax.broadcasted_iota(jnp.int32, shape, dim)


def three(v):
    hi = v.astype(bf16).astype(f32)
    mid = (v - hi).astype(bf16).astype(f32)
    lo = (v - hi - mid).astype(bf16).astype(f32)
    return hi, mid, lo


def kernel(
    gen_ref, bid_ref, rp_ref, pairs_ref, count_ref,
    gd_ref, rd_ref,
    rpf, rnorm,
    onehot, rank_row, blk_row, ebuf, tmp, xbuf, mrow, rft, gsend, gbuf, gop, colacc,
    rows, red, fin, back, back2,
    s1_send, s1_recv, ring_send, ring_recv, a_send, a_recv, b_send, b_recv,
):
    b = lax.axis_index("bucket")
    r = lax.axis_index("ref")
    x, y = r // NY, lax.rem(r, NY)
    to_b, half = r // 2, lax.rem(r, 2)
    same = to_b == b
    sames = same.astype(jnp.int32)

    bar = pltpu.get_barrier_semaphore()

    def greet(i, c):
        pl.semaphore_signal(bar, inc=1, device_id=(b, lax.rem(r + i, NR)), device_id_type=MESH)
        return c

    lax.fori_loop(1, NR, greet, 0)

    def greet_source(i, c):
        db, dr = i // 2, 2 * b + lax.rem(i, 2)

        @pl.when(jnp.logical_not((db == b) & (dr == r)))
        def _():
            pl.semaphore_signal(bar, inc=1, device_id=(db, dr), device_id_type=MESH)

        return c

    lax.fori_loop(0, NR, greet_source, 0)

    for q in range(Q):
        ebuf[q * NB:(q + 1) * NB, :] = (bid_ref[q:q + 1, :] == iota((NB, BLK), 0)).astype(f32).astype(bf16)
    i0, i1 = iota((BLK, 2 * BLK), 0), iota((BLK, 2 * BLK), 1)
    tri = ((i0 < i1) | (i1 >= BLK)).astype(f32).astype(bf16)
    sums = jnp.dot(ebuf[...], tri, preferred_element_type=f32)
    carry = jnp.zeros((NB, BLK), f32)
    for q in range(Q):
        e = ebuf[q * NB:(q + 1) * NB, :].astype(f32)
        part = sums[q * NB:(q + 1) * NB, :]
        rank = jnp.sum(e * (part[:, :BLK] + carry), axis=0, keepdims=True)
        carry = carry + part[:, BLK:]
        over = rank >= BLK
        off = jnp.where(over, rank - BLK, rank)
        rank_row[:, q * BLK:(q + 1) * BLK] = off
        blk = 2 * bid_ref[q:q + 1, :] + over.astype(jnp.int32)
        blk_row[:, q * BLK:(q + 1) * BLK] = blk
        onehot[:, q * BLK:(q + 1) * BLK] = (iota((BLK, BLK), 0) == off.astype(jnp.int32)).astype(f32).astype(bf16)

    mine = (blk_row[...] == r).astype(f32)
    picked = (gen_ref[...].astype(f32) * mine).astype(bf16)
    block = lax.dot_general(picked, onehot[...], (((1,), (1,)), ((), ())), preferred_element_type=f32)
    norm = jnp.sum(block * block, axis=0, keepdims=True)
    total = jnp.sum(jnp.where(iota((NB, BLK), 0) == to_b, carry, 0.0), axis=0, keepdims=True)
    slot_id = iota((1, BLK), 1) + half * BLK
    norm = jnp.where(slot_id.astype(f32) < total, norm, BIG)
    hi, mid, lo = three(norm)
    tmp[F:SEND, :] = jnp.zeros((SEND - F, BLK), f32)
    tmp[0:F, :] = block
    tmp[F:F + 1, :] = hi
    tmp[F + 1:F + 2, :] = mid
    tmp[F + 2:F + 3, :] = lo
    tmp[F + 3:F + 6, :] = jnp.ones((3, BLK), f32)
    gsend[...] = tmp[...].astype(bf16)

    pl.semaphore_wait(bar, 2 * NR - 1 - sames)

    t = 2 * b + half
    tx, ty = t // NY, lax.rem(t, NY)
    t_slot = ty * NX + tx

    def first(i):
        return pltpu.make_async_remote_copy(
            src_ref=gsend, dst_ref=gbuf.at[t_slot],
            send_sem=s1_send.at[i], recv_sem=s1_recv.at[tx],
            device_id=(to_b, i * NY + ty), device_id_type=MESH,
        )

    for i in range(NX):
        here = same & (x == i)

        @pl.when(jnp.logical_not(here))
        def _():
            first(i).start()

        @pl.when(here)
        def _():
            gbuf[t_slot] = gsend[...]

    kid = iota((K, PAIRS), 0) - SEND
    gid = jnp.where((kid >= 0) & (kid < NR), lax.rem(kid, NX) * NY + kid // NX, -1)
    live = iota((1, PAIRS), 1) < count_ref[0, 0]
    named = jnp.where(live, pairs_ref[0, 0, 0:1, :], -2)
    a_hot = (gid == named).astype(f32).astype(bf16)
    b_hot = (iota((NR, PAIRS), 0) == pairs_ref[0, 0, 1:2, :]).astype(f32).astype(bf16)
    listed = lax.dot_general(b_hot, a_hot, (((1,), (1,)), ((), ())), preferred_element_type=f32)
    lane = iota((NR, K), 1)
    mrow[...] = jnp.where(
        (lane >= SEND) & (lane < SEND + NR) & (listed < 0.5), BIG,
        jnp.where((lane >= F) & (lane < F + 3), 1.0, 0.0),
    )

    v = rp_ref[...].astype(f32)
    for i, part in enumerate(three(jnp.sum(v * v, axis=0))):
        rnorm[i] = part
    rpf[...] = (-2.0 * v).reshape(F * NR, BLK)
    for u in range(UN):
        xbuf[u, F:K, :] = jnp.zeros((K - F, BLK), f32)

    def prepare(first_k, c):
        for u in range(UN):
            k = first_k * UN + u
            xbuf[u, 0:F, :] = rpf[pl.ds(k, F, stride=NR), :]
            for i in range(3):
                xbuf[u, F + 3 + i:F + 4 + i, :] = rnorm[i, pl.ds(k, 1), :]
        for u in range(UN):
            k = first_k * UN + u
            at = pl.multiple_of(k * BLK, BLK)
            rft[pl.ds(at, BLK), :] = xbuf[u].astype(bf16).T + mrow[pl.ds(k, 1), :].astype(bf16)
            colacc[pl.ds(at, BLK), :] = jnp.full((BLK, BLK), 4 * BIG, f32)
        return c

    lax.fori_loop(0, NR // UN // 2, prepare, 0)

    def settle(i, slot):
        g = lax.rem(slot, NX) * NY + slot // NX
        return pltpu.make_async_remote_copy(
            src_ref=rows.at[slot], dst_ref=red.at[r],
            send_sem=a_send, recv_sem=a_recv,
            device_id=(b, g), device_id_type=MESH,
        )

    def compute(group):
        for i in range(NX):
            slot = group * NX + i
            hot = (iota((K - SEND, BLK), 0) == slot).astype(f32).astype(bf16)
            gop[0:SEND, i * BLK:(i + 1) * BLK] = gbuf[slot]
            gop[SEND:K, i * BLK:(i + 1) * BLK] = hot
        d = jnp.dot(rft[...], gop[...], preferred_element_type=f32)
        acc = jnp.min(d.reshape(NR * BLK // 8, 8, NX * BLK), axis=0)
        m = jnp.minimum(
            jnp.minimum(d[:, 0:BLK], d[:, BLK:2 * BLK]),
            jnp.minimum(d[:, 2 * BLK:3 * BLK], d[:, 3 * BLK:4 * BLK]),
        )
        colacc[...] = jnp.minimum(colacc[...], m)
        low = jnp.min(acc, axis=0, keepdims=True)
        for i in range(NX):
            slot = group * NX + i
            rows[slot] = low[:, i * BLK:(i + 1) * BLK]
        for i in range(NX):
            slot = group * NX + i
            own = (group == y) & (x == i)

            @pl.when(jnp.logical_not(own))
            def _():
                settle(i, slot).start()

            @pl.when(own)
            def _():
                red[r] = rows[slot]

    for i in range(NX):
        src_b = (i * NY + y) // 2
        here = same & (x == i)

        @pl.when(jnp.logical_not(here))
        def _():
            first(i).wait_send()
            pltpu.make_async_remote_copy(
                src_ref=gsend, dst_ref=gbuf.at[y * NX + i],
                send_sem=s1_send.at[i], recv_sem=s1_recv.at[i],
                device_id=(src_b, r), device_id_type=MESH,
            ).wait_recv()

    def ring(way, step, behind, last):
        sign = 1 - 2 * way
        group = lax.rem(y - sign * (step - behind) + 2 * NY, NY)
        if last:
            piece = gbuf.at[pl.ds(group * NX + way * (NX // 2), NX // 2)]
        else:
            piece = gbuf.at[pl.ds(group * NX, NX)]
        to = lax.rem(y + sign + NY, NY)
        return pltpu.make_async_remote_copy(
            src_ref=piece, dst_ref=piece,
            send_sem=ring_send.at[way, step - 1], recv_sem=ring_recv.at[way, step - 1],
            device_id=(b, x * NY + to), device_id_type=MESH,
        )

    for way in range(2):
        ring(way, 1, 1, False).start()
    lax.fori_loop(NR // UN // 2, NR // UN, prepare, 0)

    def group_step(i, c):
        step = (i + 1) // 2
        odd = lax.rem(i, 2)

        @pl.when((odd == 1) & (step < NY // 2))
        def _():
            for way in range(2):
                ring(way, step, 0, False).wait_recv()

                @pl.when(step + 1 < NY // 2)
                def _():
                    ring(way, step + 1, 1, False).start()

                @pl.when(step + 1 == NY // 2)
                def _():
                    ring(way, step + 1, 1, True).start()

        @pl.when(step == NY // 2)
        def _():
            for way in range(2):
                ring(way, step, 0, True).wait_recv()

        compute(lax.rem(y + (1 - 2 * odd) * step + NY, NY))
        return c

    lax.fori_loop(0, NY, group_step, 0)

    def finish(first_k, c):
        for u in range(UN):
            k = first_k * UN + u
            at = pl.multiple_of(k * BLK, BLK)
            v = colacc[pl.ds(at, BLK), :].T
            rd_ref[pl.ds(k, 1), :] = jnp.min(v, axis=0, keepdims=True) / F
        return c

    lax.fori_loop(0, NR // UN // 2, finish, 0)

    pltpu.make_async_copy(red.at[pl.ds(0, NR - 1)], red.at[pl.ds(0, NR - 1)], a_recv).wait()
    low = red[0]
    for i in range(1, NR):
        low = jnp.minimum(low, red[i])
    fin[0] = low / F

    def deliver(i, c):
        @pl.when(jnp.logical_not(same & (i == r)))
        def _():
            pltpu.make_async_remote_copy(
                src_ref=fin.at[0], dst_ref=back.at[t],
                send_sem=b_send, recv_sem=b_recv,
                device_id=(to_b, i), device_id_type=MESH,
            ).start()

        return c

    lax.fori_loop(0, NR, deliver, 0)
    lax.fori_loop(NR // UN // 2, NR // UN, finish, 0)

    @pl.when(same)
    def _():
        back[t] = fin[0]
        pltpu.make_async_copy(back.at[pl.ds(0, NR - 1)], back.at[pl.ds(0, NR - 1)], b_recv).wait()

    @pl.when(jnp.logical_not(same))
    def _():
        pltpu.make_async_copy(back.at[pl.ds(0, NR)], back.at[pl.ds(0, NR)], b_recv).wait()

    for i in range(NR):
        back2[i:i + 1, :] = back[i]
    hi, mid, lo = three(back2[...])
    parts = jnp.concatenate([hi, mid, lo], axis=0).astype(bf16)
    for q in range(0, Q, 4):
        cols = slice(q * BLK, (q + 4) * BLK)
        v = jnp.dot(parts, onehot[:, cols], preferred_element_type=f32)
        v = v[0:NR] + v[NR:2 * NR] + v[2 * NR:3 * NR]
        pick = iota((NR, 4 * BLK), 0) == blk_row[:, cols]
        v = jnp.sum(jnp.where(pick, v, 0.0), axis=0, keepdims=True)
        for i in range(4):
            gd_ref[q + i:q + i + 1, :] = v[:, i * BLK:(i + 1) * BLK]

    for way in range(2):
        for step in range(1, NY // 2 + 1):
            ring(way, step, 1, step == NY // 2).wait_send()
    pltpu.make_async_copy(rows.at[pl.ds(0, NR - 1)], rows.at[pl.ds(0, NR - 1)], a_send).wait()

    @pl.when(same)
    def _():
        pltpu.make_async_copy(back.at[pl.ds(0, NR - 1)], back.at[pl.ds(0, NR - 1)], b_send).wait()

    @pl.when(jnp.logical_not(same))
    def _():
        pltpu.make_async_copy(back.at[pl.ds(0, NR)], back.at[pl.ds(0, NR)], b_send).wait()


def per_device(gen_points, bucket_id, ref_points, block_pairs, pair_count):
    vmem = pl.BlockSpec(memory_space=pltpu.VMEM)
    dma = pltpu.SemaphoreType.DMA
    gd, rd = pl.pallas_call(
        kernel,
        out_shape=(
            jax.ShapeDtypeStruct((Q, BLK), f32),
            jax.ShapeDtypeStruct((NR, BLK), f32),
        ),
        in_specs=[vmem] * 4 + [pl.BlockSpec(memory_space=pltpu.SMEM)],
        out_specs=(vmem, vmem),
        scratch_shapes=[
            pltpu.VMEM((F * NR, BLK), f32),
            pltpu.VMEM((3, NR, BLK), f32),
            pltpu.VMEM((BLK, GEN), bf16),
            pltpu.VMEM((1, GEN), f32),
            pltpu.VMEM((1, GEN), jnp.int32),
            pltpu.VMEM((Q * NB, BLK), bf16),
            pltpu.VMEM((SEND, BLK), f32),
            pltpu.VMEM((UN, K, BLK), f32),
            pltpu.VMEM((NR, K), f32),
            pltpu.VMEM((NR * BLK, K), bf16),
            pltpu.VMEM((SEND, BLK), bf16),
            pltpu.VMEM((NR, SEND, BLK), bf16),
            pltpu.VMEM((K, NX * BLK), bf16),
            pltpu.VMEM((NR * BLK, BLK), f32),
            pltpu.VMEM((NR, 1, BLK), f32),
            pltpu.VMEM((NR, 1, BLK), f32),
            pltpu.VMEM((1, 1, BLK), f32),
            pltpu.VMEM((NR, 1, BLK), f32),
            pltpu.VMEM((NR, BLK), f32),
            dma((NX,)), dma((NX,)), dma((2, NY // 2)), dma((2, NY // 2)),
            dma, dma, dma, dma,
        ],
        compiler_params=pltpu.CompilerParams(
            collective_id=0, has_side_effects=True, vmem_limit_bytes=48 * 2**20
        ),
        cost_estimate=pl.CostEstimate(
            flops=2 * 4096 * 4096 * 128, bytes_accessed=2**21, transcendentals=0
        ),
        name="chamfer",
    )(
        gen_points, bucket_id.reshape(Q, BLK), ref_points.transpose(1, 0, 2), block_pairs,
        pair_count,
    )
    return gd.reshape(GEN), rd


def solution(mesh):
    return jax.shard_map(
        per_device,
        mesh=mesh,
        in_specs=(
            P(None, "bucket"),
            P("bucket"),
            P(("bucket", "ref"), None, None),
            P("bucket", "ref", None, None),
            P("bucket", "ref"),
        ),
        out_specs=(P("bucket"), P(("bucket", "ref"), None)),
        check_vma=False,
    )
```

```python
import jax
import jax.numpy as jnp
from jax import lax
from jax.experimental import pallas as pl
from jax.experimental.pallas import tpu as pltpu
from jax.sharding import PartitionSpec as P

F = 68
BLK = 128
NB = 16
NR = 32
NX = 4
NY = 8
GEN = 3072
Q = GEN // BLK
PAIRS = 768
SEND = 80
K = 128
UN = 8
BIG = 1e30
MESH = pl.DeviceIdType.MESH
bf16 = jnp.bfloat16
f32 = jnp.float32


def iota(shape, dim):
    return lax.broadcasted_iota(jnp.int32, shape, dim)


def three(v):
    hi = v.astype(bf16).astype(f32)
    mid = (v - hi).astype(bf16).astype(f32)
    lo = (v - hi - mid).astype(bf16).astype(f32)
    return hi, mid, lo


def kernel(
    gen_hbm, bid_hbm, rp_hbm, pairs_hbm, count_ref,
    gd_ref, rd_ref,
    gen_ref, bid_ref, rp_ref, pairs_ref, in_sem, picked,
    rpf, rnorm,
    onehot, rank_row, blk_row, ebuf, tmp, xbuf, mrow, rft, gsend, gbuf, gop, colacc,
    rows, red_y, low_y, red_x, fin, back, back2,
    s1_send, s1_recv, ring_send, ring_recv, y_send, y_recv, x_send, x_recv, z_send, z_recv,
):
    b = lax.axis_index("bucket")
    r = lax.axis_index("ref")
    x, y = r // NY, lax.rem(r, NY)
    half, turn = lax.rem(y, 2), y // 2
    mates = [4 * i + lax.rem(turn - b + NB, 4) for i in range(NX)]

    loads = [
        pltpu.make_async_copy(src, dst, in_sem.at[i])
        for i, (src, dst) in enumerate(
            [(bid_hbm, bid_ref), (gen_hbm, gen_ref), (pairs_hbm, pairs_ref), (rp_hbm, rp_ref)]
        )
    ]
    for copy in loads:
        copy.start()

    bar = pltpu.get_barrier_semaphore()

    def at_x(i):
        return (b, lax.rem(x + i, NX) * NY + y)

    def at_y(i):
        return (b, x * NY + lax.rem(y + i, NY))

    def at_z(i):
        return (lax.rem(b + i, NB), r)

    for peer, count in ((at_z, NB), (at_y, NY), (at_x, NX)):
        def greet(i, c, peer=peer):
            pl.semaphore_signal(bar, inc=1, device_id=peer(i), device_id_type=MESH)
            return c

        lax.fori_loop(1, count, greet, 0)

    loads[0].wait()
    for q in range(Q):
        ebuf[q * NB:(q + 1) * NB, :] = (bid_ref[q:q + 1, :] == iota((NB, BLK), 0)).astype(f32).astype(bf16)
    i0, i1 = iota((BLK, 2 * BLK), 0), iota((BLK, 2 * BLK), 1)
    tri = ((i0 < i1) | (i1 >= BLK)).astype(f32).astype(bf16)
    sums = jnp.dot(ebuf[...], tri, preferred_element_type=f32)
    carry = jnp.zeros((NB, BLK), f32)
    for q in range(Q):
        e = ebuf[q * NB:(q + 1) * NB, :].astype(f32)
        part = sums[q * NB:(q + 1) * NB, :]
        rank = jnp.sum(e * (part[:, :BLK] + carry), axis=0, keepdims=True)
        carry = carry + part[:, BLK:]
        over = rank >= BLK
        off = jnp.where(over, rank - BLK, rank)
        rank_row[:, q * BLK:(q + 1) * BLK] = off
        blk = 2 * bid_ref[q:q + 1, :] + over.astype(jnp.int32)
        blk_row[:, q * BLK:(q + 1) * BLK] = blk
        onehot[:, q * BLK:(q + 1) * BLK] = (iota((BLK, BLK), 0) == off.astype(jnp.int32)).astype(f32).astype(bf16)

    loads[1].wait()
    for i in range(NX):
        mine = (blk_row[...] == 2 * mates[i] + half).astype(f32).astype(bf16)
        picked[i, 0:F, :] = gen_ref[...] * mine
        picked[i, F:SEND, :] = jnp.zeros((SEND - F, GEN), bf16)
    blocks = lax.dot_general(
        picked[...].reshape(NX * SEND, GEN), onehot[...], (((1,), (1,)), ((), ())),
        preferred_element_type=f32,
    )
    for i in range(NX):
        block = blocks[i * SEND:(i + 1) * SEND]
        norm = jnp.sum(block * block, axis=0, keepdims=True)
        total = jnp.sum(jnp.where(iota((NB, BLK), 0) == mates[i], carry, 0.0), axis=0, keepdims=True)
        slot_id = iota((1, BLK), 1) + half * BLK
        norm = jnp.where(slot_id.astype(f32) < total, norm, BIG)
        tmp[i] = block
        for j, part in enumerate(three(norm)):
            tmp[i, F + j:F + j + 1, :] = part
        tmp[i, F + 3:F + 6, :] = jnp.ones((3, BLK), f32)
        gsend[i] = tmp[i].astype(bf16)

    pl.semaphore_wait(bar, NB + NX + NY - 3)

    my_slot = y * NX + b // 4

    def first(i):
        return pltpu.make_async_remote_copy(
            src_ref=gsend.at[i], dst_ref=gbuf.at[my_slot],
            send_sem=s1_send.at[i], recv_sem=s1_recv.at[b // 4],
            device_id=(mates[i], r), device_id_type=MESH,
        )

    for i in range(NX):

        @pl.when(mates[i] != b)
        def _():
            first(i).start()

        @pl.when(mates[i] == b)
        def _():
            gbuf[my_slot] = gsend[i]

    loads[2].wait()
    kid = iota((K, PAIRS), 0) - SEND
    gid = 8 * (kid & 3) + 2 * (((kid >> 3) - b + NB) & 3) + ((kid >> 2) & 1)
    gid = jnp.where((kid >= 0) & (kid < NR), gid, -1)
    live = iota((1, PAIRS), 1) < count_ref[0, 0]
    named = jnp.where(live, pairs_ref[0, 0, 0:1, :], -2)
    a_hot = (gid == named).astype(f32).astype(bf16)
    b_hot = (iota((NR, PAIRS), 0) == pairs_ref[0, 0, 1:2, :]).astype(f32).astype(bf16)
    listed = lax.dot_general(b_hot, a_hot, (((1,), (1,)), ((), ())), preferred_element_type=f32)
    lane = iota((NR, K), 1)
    mrow[...] = jnp.where(
        (lane >= SEND) & (lane < SEND + NR) & (listed < 0.5), BIG,
        jnp.where((lane >= F) & (lane < F + 3), 1.0, 0.0),
    )

    loads[3].wait()
    v = rp_ref[...].astype(f32)
    for i, part in enumerate(three(jnp.sum(v * v, axis=0))):
        rnorm[i] = part
    rpf[...] = (-2.0 * v).reshape(F * NR, BLK)
    for u in range(UN):
        xbuf[u, F:K, :] = jnp.zeros((K - F, BLK), f32)

    def prepare(first_k, c):
        for u in range(UN):
            k = first_k * UN + u
            xbuf[u, 0:F, :] = rpf[pl.ds(k, F, stride=NR), :]
            for i in range(3):
                xbuf[u, F + 3 + i:F + 4 + i, :] = rnorm[i, pl.ds(k, 1), :]
        for u in range(UN):
            k = first_k * UN + u
            at = pl.multiple_of(k * BLK, BLK)
            rft[pl.ds(at, BLK), :] = xbuf[u].astype(bf16).T + mrow[pl.ds(k, 1), :].astype(bf16)
            colacc[pl.ds(at, BLK), :] = jnp.full((BLK, BLK), 4 * BIG, f32)
        return c

    lax.fori_loop(0, NR // UN // 2, prepare, 0)

    def along_y(start, size):
        for k in range(1, NY):
            pltpu.make_async_remote_copy(
                src_ref=rows.at[pl.ds(start, size)], dst_ref=red_y.at[y, pl.ds(start, size)],
                send_sem=y_send, recv_sem=y_recv,
                device_id=at_y(k), device_id_type=MESH,
            ).start()

    def compute(i_step, group):
        for i in range(NX):
            slot = group * NX + i
            hot = (iota((K - SEND, BLK), 0) == slot).astype(f32).astype(bf16)
            gop[0:SEND, i * BLK:(i + 1) * BLK] = gbuf[slot]
            gop[SEND:K, i * BLK:(i + 1) * BLK] = hot
        d = jnp.dot(rft[...], gop[...], preferred_element_type=f32)
        acc = jnp.min(d.reshape(NR * BLK // 8, 8, NX * BLK), axis=0)
        m = jnp.minimum(
            jnp.minimum(d[:, 0:BLK], d[:, BLK:2 * BLK]),
            jnp.minimum(d[:, 2 * BLK:3 * BLK], d[:, 3 * BLK:4 * BLK]),
        )
        colacc[...] = jnp.minimum(colacc[...], m)
        low = jnp.min(acc, axis=0, keepdims=True)
        for i in range(NX):
            rows[i_step * NX + i] = low[:, i * BLK:(i + 1) * BLK]

    for i in range(NX):

        @pl.when(mates[i] != b)
        def _():
            first(i).wait_send()
            pltpu.make_async_remote_copy(
                src_ref=gsend.at[i], dst_ref=gbuf.at[y * NX + i],
                send_sem=s1_send.at[i], recv_sem=s1_recv.at[i],
                device_id=(mates[i], r), device_id_type=MESH,
            ).wait_recv()

    def ring(way, step, behind, last):
        sign = 1 - 2 * way
        group = lax.rem(y - sign * (step - behind) + 2 * NY, NY)
        if last:
            piece = gbuf.at[pl.ds(group * NX + way * (NX // 2), NX // 2)]
        else:
            piece = gbuf.at[pl.ds(group * NX, NX)]
        to = lax.rem(y + sign + NY, NY)
        return pltpu.make_async_remote_copy(
            src_ref=piece, dst_ref=piece,
            send_sem=ring_send.at[way, step - 1], recv_sem=ring_recv.at[way, step - 1],
            device_id=(b, x * NY + to), device_id_type=MESH,
        )

    for way in range(2):
        ring(way, 1, 1, False).start()
    lax.fori_loop(NR // UN // 2, NR // UN, prepare, 0)

    def group_step(i, c):
        step = (i + 1) // 2
        odd = lax.rem(i, 2)

        @pl.when((odd == 1) & (step < NY // 2))
        def _():
            for way in range(2):
                ring(way, step, 0, False).wait_recv()

                @pl.when(step + 1 < NY // 2)
                def _():
                    ring(way, step + 1, 1, False).start()

                @pl.when(step + 1 == NY // 2)
                def _():
                    ring(way, step + 1, 1, True).start()

        @pl.when(step == NY // 2)
        def _():
            for way in range(2):
                ring(way, step, 0, True).wait_recv()

        compute(i, lax.rem(y + (1 - 2 * odd) * step + NY, NY))

        @pl.when(i == 5)
        def _():
            along_y(0, 6 * NX)

        @pl.when(i == 7)
        def _():
            along_y(6 * NX, 2 * NX)

        return c

    lax.fori_loop(0, NY, group_step, 0)

    def finish(first_k, c):
        for u in range(UN):
            k = first_k * UN + u
            at = pl.multiple_of(k * BLK, BLK)
            v = colacc[pl.ds(at, BLK), :].T
            rd_ref[pl.ds(k, 1), :] = jnp.min(v, axis=0, keepdims=True) / F
        return c

    lax.fori_loop(0, NR // UN // 2, finish, 0)

    pltpu.make_async_copy(red_y.at[pl.ds(0, NY - 1)], red_y.at[pl.ds(0, NY - 1)], y_recv).wait()
    order = {0: 0, 7: 1, 1: 2, 6: 3, 2: 4, 5: 5, 3: 6, 4: 7}
    for ahead in range(NY):
        at = order[ahead] * NX
        low = rows[at:at + NX]
        for k in range(1, NY):
            at = order[(ahead - k) % NY] * NX
            low = jnp.minimum(low, red_y[lax.rem(y + k, NY), at:at + NX])
        low_y[pl.ds(lax.rem(y + ahead, NY) * NX, NX)] = low

    for k in range(1, NX):
        pltpu.make_async_remote_copy(
            src_ref=low_y, dst_ref=red_x.at[x],
            send_sem=x_send, recv_sem=x_recv, device_id=at_x(k), device_id_type=MESH,
        ).start()
    lax.fori_loop(NR // UN // 2, NR // UN, finish, 0)
    pltpu.make_async_copy(red_x.at[pl.ds(0, NX - 1)], red_x.at[pl.ds(0, NX - 1)], x_recv).wait()
    for s in range(NB):
        for h in range(2):
            slot = (2 * lax.rem(b + s, 4) + h) * NX + s // 4
            low = low_y[slot]
            for k in range(1, NX):
                low = jnp.minimum(low, red_x[lax.rem(x + k, NX), slot])
            fin[2 * s + h] = low / F

    def deliver(i, c):
        s = lax.rem(b + i, NB)
        pltpu.make_async_remote_copy(
            src_ref=fin.at[pl.ds(2 * s, 2)], dst_ref=back.at[pl.ds(2 * b, 2)],
            send_sem=z_send, recv_sem=z_recv, device_id=(s, r), device_id_type=MESH,
        ).start()
        return c

    lax.fori_loop(1, NB, deliver, 0)
    back[pl.ds(2 * b, 2)] = fin[pl.ds(2 * b, 2)]
    pltpu.make_async_copy(back.at[pl.ds(0, NR - 2)], back.at[pl.ds(0, NR - 2)], z_recv).wait()

    for i in range(NR):
        back2[i:i + 1, :] = back[i]
    hi, mid, lo = three(back2[...])
    parts = jnp.concatenate([hi, mid, lo], axis=0).astype(bf16)
    for q in range(0, Q, 4):
        cols = slice(q * BLK, (q + 4) * BLK)
        v = jnp.dot(parts, onehot[:, cols], preferred_element_type=f32)
        v = v[0:NR] + v[NR:2 * NR] + v[2 * NR:3 * NR]
        pick = iota((NR, 4 * BLK), 0) == blk_row[:, cols]
        v = jnp.sum(jnp.where(pick, v, 0.0), axis=0, keepdims=True)
        for i in range(4):
            gd_ref[q + i:q + i + 1, :] = v[:, i * BLK:(i + 1) * BLK]

    for way in range(2):
        for step in range(1, NY // 2 + 1):
            ring(way, step, 1, step == NY // 2).wait_send()
    pltpu.make_async_copy(red_y.at[pl.ds(0, NY - 1)], red_y.at[pl.ds(0, NY - 1)], y_send).wait()
    pltpu.make_async_copy(red_x.at[pl.ds(0, NX - 1)], red_x.at[pl.ds(0, NX - 1)], x_send).wait()
    pltpu.make_async_copy(back.at[pl.ds(0, NR - 2)], back.at[pl.ds(0, NR - 2)], z_send).wait()


def per_device(gen_points, bucket_id, ref_points, block_pairs, pair_count):
    vmem = pl.BlockSpec(memory_space=pltpu.VMEM)
    dma = pltpu.SemaphoreType.DMA
    gd, rd = pl.pallas_call(
        kernel,
        out_shape=(
            jax.ShapeDtypeStruct((Q, BLK), f32),
            jax.ShapeDtypeStruct((NR, BLK), f32),
        ),
        in_specs=[pl.BlockSpec(memory_space=pltpu.HBM)] * 4 + [pl.BlockSpec(memory_space=pltpu.SMEM)],
        out_specs=(vmem, vmem),
        scratch_shapes=[
            pltpu.VMEM((F, GEN), bf16),
            pltpu.VMEM((Q, BLK), jnp.int32),
            pltpu.VMEM((F, NR, BLK), bf16),
            pltpu.VMEM((1, 1, 2, PAIRS), jnp.int32),
            dma((4,)),
            pltpu.VMEM((NX, SEND, GEN), bf16),
            pltpu.VMEM((F * NR, BLK), f32),
            pltpu.VMEM((3, NR, BLK), f32),
            pltpu.VMEM((BLK, GEN), bf16),
            pltpu.VMEM((1, GEN), f32),
            pltpu.VMEM((1, GEN), jnp.int32),
            pltpu.VMEM((Q * NB, BLK), bf16),
            pltpu.VMEM((NX, SEND, BLK), f32),
            pltpu.VMEM((UN, K, BLK), f32),
            pltpu.VMEM((NR, K), f32),
            pltpu.VMEM((NR * BLK, K), bf16),
            pltpu.VMEM((NX, SEND, BLK), bf16),
            pltpu.VMEM((NR, SEND, BLK), bf16),
            pltpu.VMEM((K, NX * BLK), bf16),
            pltpu.VMEM((NR * BLK, BLK), f32),
            pltpu.VMEM((NR, 1, BLK), f32),
            pltpu.VMEM((NY, NR, 1, BLK), f32),
            pltpu.VMEM((NR, 1, BLK), f32),
            pltpu.VMEM((NX, NR, 1, BLK), f32),
            pltpu.VMEM((NR, 1, BLK), f32),
            pltpu.VMEM((NR, 1, BLK), f32),
            pltpu.VMEM((NR, BLK), f32),
            dma((NX,)), dma((NX,)), dma((2, NY // 2)), dma((2, NY // 2)),
            dma, dma, dma, dma, dma, dma,
        ],
        compiler_params=pltpu.CompilerParams(
            collective_id=0, has_side_effects=True, vmem_limit_bytes=56 * 2**20
        ),
        cost_estimate=pl.CostEstimate(
            flops=2 * 4096 * 4096 * 128, bytes_accessed=2**21, transcendentals=0
        ),
        name="chamfer",
    )(
        gen_points, bucket_id.reshape(Q, BLK), ref_points.transpose(1, 0, 2), block_pairs,
        pair_count,
    )
    return gd.reshape(GEN), rd


def solution(mesh):
    return jax.shard_map(
        per_device,
        mesh=mesh,
        in_specs=(
            P(None, "bucket"),
            P("bucket"),
            P(("bucket", "ref"), None, None),
            P("bucket", "ref", None, None),
            P("bucket", "ref"),
        ),
        out_specs=(P("bucket"), P(("bucket", "ref"), None)),
        check_vma=False,
    )
```

```python
import jax
import jax.numpy as jnp
from jax import lax
from jax.experimental import pallas as pl
from jax.experimental.pallas import tpu as pltpu
from jax.sharding import PartitionSpec as P

F = 68
BLK = 128
NB = 16
NR = 32
NX = 4
NY = 8
GEN = 3072
Q = GEN // BLK
PAIRS = 768
SEND = 80
K = 128
UN = 8
BIG = 1e30
MESH = pl.DeviceIdType.MESH
bf16 = jnp.bfloat16
f32 = jnp.float32


def iota(shape, dim):
    return lax.broadcasted_iota(jnp.int32, shape, dim)


def three(v):
    hi = v.astype(bf16).astype(f32)
    mid = (v - hi).astype(bf16).astype(f32)
    lo = (v - hi - mid).astype(bf16).astype(f32)
    return hi, mid, lo


def kernel(
    gen_hbm, bid_hbm, rp_hbm, pairs_hbm, count_ref,
    gd_ref, rd_ref,
    gen_ref, bid_ref, rp_ref, pairs_ref, in_sem, picked,
    rpf, rnorm,
    onehot, rank_row, blk_row, ebuf, tmp, xbuf, mrow, rft, gsend, gbuf, gop, colacc,
    rows, red_y, fin, back, sized, back2,
    s1_send, s1_recv, ring_send, ring_recv, y_send, y_recv, z_send, z_recv, known,
):
    b = lax.axis_index("bucket")
    r = lax.axis_index("ref")
    x, y = r // NY, lax.rem(r, NY)
    mates = [4 * i + lax.rem(x - b + NB, 4) for i in range(NX)]

    bar = pltpu.get_barrier_semaphore()

    def at_x(i):
        return (b, lax.rem(x + i, NX) * NY + y)

    def at_y(i):
        return (b, x * NY + lax.rem(y + i, NY))

    def at_z(i):
        return (lax.rem(b + i, NB), r)

    def far_first(j, count):
        return count // 2 + (j // 2) * (1 - lax.rem(j, 2)) - (j // 2 + 1) * lax.rem(j, 2)

    for peer, count in ((at_z, NB), (at_y, NY), (at_x, NX)):
        def greet(j, c, peer=peer, count=count):
            to = peer(far_first(j, count))
            pl.semaphore_signal(bar, inc=1, device_id=to, device_id_type=MESH)
            return c

        lax.fori_loop(0, count - 1, greet, 0)

    loads = [
        pltpu.make_async_copy(src, dst, in_sem.at[i])
        for i, (src, dst) in enumerate(
            [(bid_hbm, bid_ref), (gen_hbm, gen_ref), (pairs_hbm, pairs_ref), (rp_hbm, rp_ref)]
        )
    ]
    for copy in loads:
        copy.start()

    loads[0].wait()
    for q in range(Q):
        ebuf[q * NB:(q + 1) * NB, :] = (bid_ref[q:q + 1, :] == iota((NB, BLK), 0)).astype(f32).astype(bf16)
    i0, i1 = iota((BLK, 2 * BLK), 0), iota((BLK, 2 * BLK), 1)
    tri = ((i0 < i1) | (i1 >= BLK)).astype(f32).astype(bf16)
    sums = jnp.dot(ebuf[...], tri, preferred_element_type=f32)
    carry = jnp.zeros((NB, BLK), f32)
    for q in range(Q):
        e = ebuf[q * NB:(q + 1) * NB, :].astype(f32)
        part = sums[q * NB:(q + 1) * NB, :]
        rank = jnp.sum(e * (part[:, :BLK] + carry), axis=0, keepdims=True)
        carry = carry + part[:, BLK:]
        over = rank >= BLK
        off = jnp.where(over, rank - BLK, rank)
        rank_row[:, q * BLK:(q + 1) * BLK] = off
        blk = 2 * bid_ref[q:q + 1, :] + over.astype(jnp.int32)
        blk_row[:, q * BLK:(q + 1) * BLK] = blk
        onehot[:, q * BLK:(q + 1) * BLK] = (iota((BLK, BLK), 0) == off.astype(jnp.int32)).astype(f32).astype(bf16)

    def first(i, u):
        slot = (2 * x + u) * NX + b // 4
        return pltpu.make_async_remote_copy(
            src_ref=gsend.at[u, i], dst_ref=gbuf.at[slot],
            send_sem=s1_send.at[u, i], recv_sem=s1_recv.at[u, b // 4],
            device_id=(mates[i], r), device_id_type=MESH,
        )

    loads[1].wait()
    for i in range(NX):
        picked[i, F:SEND, :] = jnp.zeros((SEND - F, GEN), bf16)
    for u in range(2):
        for i in range(NX):
            mine = (blk_row[...] == 2 * mates[i] + u).astype(f32).astype(bf16)
            picked[i, 0:F, :] = gen_ref[...] * mine
        blocks = lax.dot_general(
            picked[...].reshape(NX * SEND, GEN), onehot[...], (((1,), (1,)), ((), ())),
            preferred_element_type=f32,
        )
        for i in range(NX):
            block = blocks[i * SEND:(i + 1) * SEND]
            norm = jnp.sum(block * block, axis=0, keepdims=True)
            total = jnp.sum(
                jnp.where(iota((NB, BLK), 0) == mates[i], carry, 0.0), axis=0, keepdims=True
            )
            slot_id = iota((1, BLK), 1) + u * BLK
            norm = jnp.where(slot_id.astype(f32) < total, norm, BIG)
            tmp[i] = block
            for j, part in enumerate(three(norm)):
                tmp[i, F + j:F + j + 1, :] = part
            tmp[i, F + 3:F + 6, :] = jnp.ones((3, BLK), f32)
            gsend[u, i] = tmp[i].astype(bf16)

        if u == 0:
            pl.semaphore_wait(bar, NB + NX + NY - 3)
            for k in range(1, NX):
                pl.semaphore_signal(known, inc=1, device_id=at_x(k), device_id_type=MESH)

        for i in range(NX):

            @pl.when(mates[i] != b)
            def _():
                first(i, u).start()

            @pl.when(mates[i] == b)
            def _():
                gbuf[(2 * x + u) * NX + b // 4] = gsend[u, i]

    loads[2].wait()
    kid = iota((K, PAIRS), 0) - SEND
    gid = 8 * (kid & 3) + 2 * (((kid >> 3) - b + NB) & 3) + ((kid >> 2) & 1)
    gid = jnp.where((kid >= 0) & (kid < NR), gid, -1)
    live = iota((1, PAIRS), 1) < count_ref[0, 0]
    named = jnp.where(live, pairs_ref[0, 0, 0:1, :], -2)
    a_hot = (gid == named).astype(f32).astype(bf16)
    b_hot = (iota((NR, PAIRS), 0) == pairs_ref[0, 0, 1:2, :]).astype(f32).astype(bf16)
    listed = lax.dot_general(b_hot, a_hot, (((1,), (1,)), ((), ())), preferred_element_type=f32)
    lane = iota((NR, K), 1)
    mrow[...] = jnp.where(
        (lane >= SEND) & (lane < SEND + NR) & (listed < 0.5), BIG,
        jnp.where((lane >= F) & (lane < F + 3), 1.0, 0.0),
    )

    loads[3].wait()
    v = rp_ref[...].astype(f32)
    for i, part in enumerate(three(jnp.sum(v * v, axis=0))):
        rnorm[i] = part
    rpf[...] = (-2.0 * v).reshape(F * NR, BLK)
    for u in range(UN):
        xbuf[u, F:K, :] = jnp.zeros((K - F, BLK), f32)

    def prepare(first_k, c):
        for u in range(UN):
            k = first_k * UN + u
            xbuf[u, 0:F, :] = rpf[pl.ds(k, F, stride=NR), :]
            for i in range(3):
                xbuf[u, F + 3 + i:F + 4 + i, :] = rnorm[i, pl.ds(k, 1), :]
        for u in range(UN):
            k = first_k * UN + u
            at = pl.multiple_of(k * BLK, BLK)
            rft[pl.ds(at, BLK), :] = xbuf[u].astype(bf16).T + mrow[pl.ds(k, 1), :].astype(bf16)
            colacc[pl.ds(at, BLK), :] = jnp.full((BLK, BLK), 4 * BIG, f32)
        return c

    lax.fori_loop(0, NR // UN // 2, prepare, 0)

    def along_y(start, size):
        for k in (4, 3, 5, 2, 6, 1, 7):
            pltpu.make_async_remote_copy(
                src_ref=rows.at[pl.ds(start, size)], dst_ref=red_y.at[y, pl.ds(start, size)],
                send_sem=y_send, recv_sem=y_recv,
                device_id=at_y(k), device_id_type=MESH,
            ).start()

    def compute(i_step, group):
        for i in range(NX):
            slot = group * NX + i
            hot = (iota((K - SEND, BLK), 0) == slot).astype(f32).astype(bf16)
            gop[0:SEND, i * BLK:(i + 1) * BLK] = gbuf[slot]
            gop[SEND:K, i * BLK:(i + 1) * BLK] = hot
        d = jnp.dot(rft[...], gop[...], preferred_element_type=f32)
        acc = jnp.min(d.reshape(NR * BLK // 8, 8, NX * BLK), axis=0)
        m = jnp.minimum(
            jnp.minimum(d[:, 0:BLK], d[:, BLK:2 * BLK]),
            jnp.minimum(d[:, 2 * BLK:3 * BLK], d[:, 3 * BLK:4 * BLK]),
        )
        colacc[...] = jnp.minimum(colacc[...], m)
        low = jnp.min(acc, axis=0, keepdims=True)
        for i in range(NX):
            rows[i_step * NX + i] = low[:, i * BLK:(i + 1) * BLK]

    def own_arrived(u):
        for i in range(NX):

            @pl.when(mates[i] != b)
            def _():
                pltpu.make_async_remote_copy(
                    src_ref=gsend.at[u, i], dst_ref=gbuf.at[(2 * x + u) * NX + i],
                    send_sem=s1_send.at[u, i], recv_sem=s1_recv.at[u, i],
                    device_id=(mates[i], r), device_id_type=MESH,
                ).wait_recv()

    def ring(way, u, step, behind):
        sign = 1 - 2 * way
        group = 2 * lax.rem(x - sign * (step - behind) + NX, NX) + u
        if step == 2:
            piece = gbuf.at[pl.ds(group * NX + way * (NX // 2), NX // 2)]
        else:
            piece = gbuf.at[pl.ds(group * NX, NX)]
        return pltpu.make_async_remote_copy(
            src_ref=piece, dst_ref=piece,
            send_sem=ring_send.at[way, u, step - 1], recv_sem=ring_recv.at[way, u, step - 1],
            device_id=at_x(sign + NX), device_id_type=MESH,
        )

    def leave(u):
        own_arrived(u)
        for way in range(2):
            ring(way, u, 1, 1).start()

    def pass_on(u):
        for way in range(2):
            ring(way, u, 1, 0).wait_recv()
            ring(way, u, 2, 1).start()

    def last_arrived(u):
        for way in range(2):
            ring(way, u, 2, 0).wait_recv()

    leave(0)
    lax.fori_loop(NR // UN // 2, NR // UN, prepare, 0)
    leave(1)

    def group_step(i, c):
        for at, what, u in ((2, pass_on, 0), (4, pass_on, 1), (6, last_arrived, 0), (7, last_arrived, 1)):

            @pl.when(i == at)
            def _():
                what(u)

        near = (i > 1) & (i < 6)
        u = jnp.where(near, (i - 2) // 2, lax.rem(i, 2))
        away = jnp.where(near, 3 - 2 * lax.rem(i, 2), jnp.where(i < 2, 0, 2))
        compute(i, 2 * lax.rem(x + away, NX) + u)

        @pl.when(i == 5)
        def _():
            along_y(0, 6 * NX)

        @pl.when(i == 7)
        def _():
            along_y(6 * NX, 2 * NX)

        return c

    lax.fori_loop(0, NY, group_step, 0)

    def finish(first_k, c):
        for u in range(UN):
            k = first_k * UN + u
            at = pl.multiple_of(k * BLK, BLK)
            v = colacc[pl.ds(at, BLK), :].T
            rd_ref[pl.ds(k, 1), :] = jnp.min(v, axis=0, keepdims=True) / F
        return c

    lax.fori_loop(0, NR // UN // 2, finish, 0)

    pltpu.make_async_copy(red_y.at[pl.ds(0, NY - 1)], red_y.at[pl.ds(0, NY - 1)], y_recv).wait()
    for i in range(2 * NX):
        at = i * NX
        low = rows[at:at + NX]
        for k in range(1, NY):
            low = jnp.minimum(low, red_y[lax.rem(y + k, NY), at:at + NX])
        u = (i - 2) // 2 if 1 < i < 6 else i % 2
        away = 3 - 2 * (i % 2) if 1 < i < 6 else (0 if i < 2 else 2)
        first_s = lax.rem(x + away - b + NB, 4)
        for j in range(NX):
            fin[2 * (4 * j + first_s) + u] = low[j]

    pl.semaphore_wait(known, NX - 1)

    def deliver(j, c):
        off = far_first(j, NB)
        s = lax.rem(b + off, NB)
        for k in (2, 1, 3, 0):

            @pl.when((off != 0) | (k != 0))
            def _():
                pltpu.make_async_remote_copy(
                    src_ref=fin.at[pl.ds(2 * s, 2)], dst_ref=back.at[x, pl.ds(2 * b, 2)],
                    send_sem=z_send, recv_sem=z_recv,
                    device_id=(s, lax.rem(x + k, NX) * NY + y), device_id_type=MESH,
                ).start()

        return c

    lax.fori_loop(0, NB, deliver, 0)
    back[x, pl.ds(2 * b, 2)] = fin[pl.ds(2 * b, 2)]
    lax.fori_loop(NR // UN // 2, NR // UN, finish, 0)
    pltpu.make_async_copy(sized, sized, z_recv).wait()

    for i in range(NR):
        low = jnp.minimum(jnp.minimum(back[0, i], back[1, i]), jnp.minimum(back[2, i], back[3, i]))
        back2[i:i + 1, :] = low / F
    hi, mid, lo = three(back2[...])
    parts = jnp.concatenate([hi, mid, lo], axis=0).astype(bf16)
    for q in range(0, Q, 4):
        cols = slice(q * BLK, (q + 4) * BLK)
        v = jnp.dot(parts, onehot[:, cols], preferred_element_type=f32)
        v = v[0:NR] + v[NR:2 * NR] + v[2 * NR:3 * NR]
        pick = iota((NR, 4 * BLK), 0) == blk_row[:, cols]
        v = jnp.sum(jnp.where(pick, v, 0.0), axis=0, keepdims=True)
        for i in range(4):
            gd_ref[q + i:q + i + 1, :] = v[:, i * BLK:(i + 1) * BLK]

    for u in range(2):
        for i in range(NX):

            @pl.when(mates[i] != b)
            def _():
                first(i, u).wait_send()

        for way in range(2):
            for step in (1, 2):
                ring(way, u, step, 1).wait_send()
    pltpu.make_async_copy(red_y.at[0:NY - 1], red_y.at[0:NY - 1], y_send).wait()
    pltpu.make_async_copy(sized, sized, z_send).wait()


def per_device(gen_points, bucket_id, ref_points, block_pairs, pair_count):
    vmem = pl.BlockSpec(memory_space=pltpu.VMEM)
    dma = pltpu.SemaphoreType.DMA
    gd, rd = pl.pallas_call(
        kernel,
        out_shape=(
            jax.ShapeDtypeStruct((Q, BLK), f32),
            jax.ShapeDtypeStruct((NR, BLK), f32),
        ),
        in_specs=[pl.BlockSpec(memory_space=pltpu.HBM)] * 4 + [pl.BlockSpec(memory_space=pltpu.SMEM)],
        out_specs=(vmem, vmem),
        scratch_shapes=[
            pltpu.VMEM((F, GEN), bf16),
            pltpu.VMEM((Q, BLK), jnp.int32),
            pltpu.VMEM((F, NR, BLK), bf16),
            pltpu.VMEM((1, 1, 2, PAIRS), jnp.int32),
            dma((4,)),
            pltpu.VMEM((NX, SEND, GEN), bf16),
            pltpu.VMEM((F * NR, BLK), f32),
            pltpu.VMEM((3, NR, BLK), f32),
            pltpu.VMEM((BLK, GEN), bf16),
            pltpu.VMEM((1, GEN), f32),
            pltpu.VMEM((1, GEN), jnp.int32),
            pltpu.VMEM((Q * NB, BLK), bf16),
            pltpu.VMEM((NX, SEND, BLK), f32),
            pltpu.VMEM((UN, K, BLK), f32),
            pltpu.VMEM((NR, K), f32),
            pltpu.VMEM((NR * BLK, K), bf16),
            pltpu.VMEM((2, NX, SEND, BLK), bf16),
            pltpu.VMEM((NR, SEND, BLK), bf16),
            pltpu.VMEM((K, NX * BLK), bf16),
            pltpu.VMEM((NR * BLK, BLK), f32),
            pltpu.VMEM((NR, 1, BLK), f32),
            pltpu.VMEM((NY, NR, 1, BLK), f32),
            pltpu.VMEM((NR, 1, BLK), f32),
            pltpu.VMEM((NX, NR, 1, BLK), f32),
            pltpu.VMEM((NX * NR - 2, 1, BLK), f32),
            pltpu.VMEM((NR, BLK), f32),
            dma((2, NX)), dma((2, NX)), dma((2, 2, 2)), dma((2, 2, 2)),
            dma, dma, dma, dma, pltpu.SemaphoreType.REGULAR,
        ],
        compiler_params=pltpu.CompilerParams(
            collective_id=0, has_side_effects=True, vmem_limit_bytes=56 * 2**20
        ),
        cost_estimate=pl.CostEstimate(
            flops=2 * 4096 * 4096 * 128, bytes_accessed=2**21, transcendentals=0
        ),
        name="chamfer",
    )(
        gen_points, bucket_id.reshape(Q, BLK), ref_points.transpose(1, 0, 2), block_pairs,
        pair_count,
    )
    return gd.reshape(GEN), rd


def solution(mesh):
    return jax.shard_map(
        per_device,
        mesh=mesh,
        in_specs=(
            P(None, "bucket"),
            P("bucket"),
            P(("bucket", "ref"), None, None),
            P("bucket", "ref", None, None),
            P("bucket", "ref"),
        ),
        out_specs=(P("bucket"), P(("bucket", "ref"), None)),
        check_vma=False,
    )
```

```python
import jax
import jax.numpy as jnp
from jax import lax
from jax.experimental import pallas as pl
from jax.experimental.pallas import tpu as pltpu
from jax.sharding import PartitionSpec as P

F = 68
BLK = 128
NB = 16
NR = 32
NX = 4
NY = 8
GEN = 3072
Q = GEN // BLK
PAIRS = 768
SEND = 80
K = 128
UN = 8
BIG = 1e30
MESH = pl.DeviceIdType.MESH
bf16 = jnp.bfloat16
f32 = jnp.float32


def iota(shape, dim):
    return lax.broadcasted_iota(jnp.int32, shape, dim)


def three(v):
    hi = v.astype(bf16).astype(f32)
    mid = (v - hi).astype(bf16).astype(f32)
    lo = (v - hi - mid).astype(bf16).astype(f32)
    return hi, mid, lo


def kernel(
    gen_hbm, bid_hbm, rp_hbm, pairs_hbm, count_ref,
    gd_ref, rd_ref,
    gen_ref, bid_ref, rp_ref, pairs_ref, in_sem, picked,
    rpf, rnorm,
    onehot, rank_row, blk_row, ebuf, tmp, xbuf, mrow, rft, gsend, gbuf, gop, colacc,
    rows, red_y, fin, back, sized, back2,
    s1_send, s1_recv, ring_send, ring_recv, y_send, y_recv, z_send, z_recv, known,
):
    b = lax.axis_index("bucket")
    r = lax.axis_index("ref")
    x, y = r // NY, lax.rem(r, NY)
    def quarter(k, c):
        return 4 * lax.rem(b // 4 + k, 4) + c

    def source(at_x, u, a):
        c = lax.rem(at_x - b + NB, 4)
        k = jnp.where(c // 2 - lax.rem(b, 4) // 2 == 1, 3, 1)
        return quarter(2 * u if a == 0 else (4 - k if u else k), c)

    def target(u, a):
        c = lax.rem(x - b + NB, 4)
        k = jnp.where(c // 2 - lax.rem(b, 4) // 2 == -1, 1, 3)
        return quarter(2 * u if a == 0 else (4 - k if u else k), c)

    bar = pltpu.get_barrier_semaphore()

    def at_x(i):
        return (b, lax.rem(x + i, NX) * NY + y)

    def at_y(i):
        return (b, x * NY + lax.rem(y + i, NY))

    def at_z(i):
        return (lax.rem(b + i, NB), r)

    def far_first(j, count):
        return count // 2 + (j // 2) * (1 - lax.rem(j, 2)) - (j // 2 + 1) * lax.rem(j, 2)

    for peer, count in ((at_z, NB), (at_y, NY), (at_x, NX)):
        def greet(j, c, peer=peer, count=count):
            to = peer(far_first(j, count))
            pl.semaphore_signal(bar, inc=1, device_id=to, device_id_type=MESH)
            return c

        lax.fori_loop(0, count - 1, greet, 0)

    loads = [
        pltpu.make_async_copy(src, dst, in_sem.at[i])
        for i, (src, dst) in enumerate(
            [(bid_hbm, bid_ref), (gen_hbm, gen_ref), (pairs_hbm, pairs_ref), (rp_hbm, rp_ref)]
        )
    ]
    for copy in loads:
        copy.start()

    loads[0].wait()
    for q in range(Q):
        ebuf[q * NB:(q + 1) * NB, :] = (bid_ref[q:q + 1, :] == iota((NB, BLK), 0)).astype(f32).astype(bf16)
    i0, i1 = iota((BLK, 2 * BLK), 0), iota((BLK, 2 * BLK), 1)
    tri = ((i0 < i1) | (i1 >= BLK)).astype(f32).astype(bf16)
    sums = jnp.dot(ebuf[...], tri, preferred_element_type=f32)
    carry = jnp.zeros((NB, BLK), f32)
    for q in range(Q):
        e = ebuf[q * NB:(q + 1) * NB, :].astype(f32)
        part = sums[q * NB:(q + 1) * NB, :]
        rank = jnp.sum(e * (part[:, :BLK] + carry), axis=0, keepdims=True)
        carry = carry + part[:, BLK:]
        over = rank >= BLK
        off = jnp.where(over, rank - BLK, rank)
        rank_row[:, q * BLK:(q + 1) * BLK] = off
        blk = 2 * bid_ref[q:q + 1, :] + over.astype(jnp.int32)
        blk_row[:, q * BLK:(q + 1) * BLK] = blk
        onehot[:, q * BLK:(q + 1) * BLK] = (iota((BLK, BLK), 0) == off.astype(jnp.int32)).astype(f32).astype(bf16)

    def first(u, a):
        return pltpu.make_async_remote_copy(
            src_ref=gsend.at[u, a], dst_ref=gbuf.at[pl.ds((2 * x + u) * NX + 2 * a, 2)],
            send_sem=s1_send.at[u, a], recv_sem=s1_recv.at[u, a],
            device_id=(target(u, a), r), device_id_type=MESH,
        )

    loads[1].wait()
    for i in range(NX):
        picked[i, F:SEND, :] = jnp.zeros((SEND - F, GEN), bf16)
    for u in range(2):
        for i in range(NX):
            mine = (blk_row[...] == 2 * target(u, i // 2) + i % 2).astype(f32).astype(bf16)
            picked[i, 0:F, :] = gen_ref[...] * mine
        blocks = lax.dot_general(
            picked[...].reshape(NX * SEND, GEN), onehot[...], (((1,), (1,)), ((), ())),
            preferred_element_type=f32,
        )
        for i in range(NX):
            block = blocks[i * SEND:(i + 1) * SEND]
            norm = jnp.sum(block * block, axis=0, keepdims=True)
            total = jnp.sum(
                jnp.where(iota((NB, BLK), 0) == target(u, i // 2), carry, 0.0), axis=0, keepdims=True
            )
            slot_id = iota((1, BLK), 1) + (i % 2) * BLK
            norm = jnp.where(slot_id.astype(f32) < total, norm, BIG)
            tmp[i] = block
            for j, part in enumerate(three(norm)):
                tmp[i, F + j:F + j + 1, :] = part
            tmp[i, F + 3:F + 6, :] = jnp.ones((3, BLK), f32)
            gsend[u, i // 2, i % 2] = tmp[i].astype(bf16)

        if u == 0:
            pl.semaphore_wait(bar, NB + NX + NY - 3)
            for k in range(1, NX):
                pl.semaphore_signal(known, inc=1, device_id=at_x(k), device_id_type=MESH)

        for a in range(2):

            @pl.when(target(u, a) != b)
            def _():
                first(u, a).start()

            @pl.when(target(u, a) == b)
            def _():
                gbuf[pl.ds((2 * x + u) * NX + 2 * a, 2)] = gsend[u, a]

    loads[2].wait()
    kid = iota((K, PAIRS), 0) - SEND
    c = ((kid >> 3) - b + NB) & 3
    k = jnp.where((c >> 1) - lax.rem(b, 4) // 2 == 1, 3, 1)
    far = ((kid >> 2) & 1) == 1
    k = jnp.where((kid & 2) == 0, jnp.where(far, 2, 0), jnp.where(far, 4 - k, k))
    gid = 8 * ((b // 4 + k) & 3) + 2 * c + (kid & 1)
    gid = jnp.where((kid >= 0) & (kid < NR), gid, -1)
    live = iota((1, PAIRS), 1) < count_ref[0, 0]
    named = jnp.where(live, pairs_ref[0, 0, 0:1, :], -2)
    a_hot = (gid == named).astype(f32).astype(bf16)
    b_hot = (iota((NR, PAIRS), 0) == pairs_ref[0, 0, 1:2, :]).astype(f32).astype(bf16)
    listed = lax.dot_general(b_hot, a_hot, (((1,), (1,)), ((), ())), preferred_element_type=f32)
    lane = iota((NR, K), 1)
    mrow[...] = jnp.where(
        (lane >= SEND) & (lane < SEND + NR) & (listed < 0.5), BIG,
        jnp.where((lane >= F) & (lane < F + 3), 1.0, 0.0),
    )

    loads[3].wait()
    v = rp_ref[...].astype(f32)
    for i, part in enumerate(three(jnp.sum(v * v, axis=0))):
        rnorm[i] = part
    rpf[...] = (-2.0 * v).reshape(F * NR, BLK)
    for u in range(UN):
        xbuf[u, F:K, :] = jnp.zeros((K - F, BLK), f32)

    def prepare(first_k, c):
        for u in range(UN):
            k = first_k * UN + u
            xbuf[u, 0:F, :] = rpf[pl.ds(k, F, stride=NR), :]
            for i in range(3):
                xbuf[u, F + 3 + i:F + 4 + i, :] = rnorm[i, pl.ds(k, 1), :]
        for u in range(UN):
            k = first_k * UN + u
            at = pl.multiple_of(k * BLK, BLK)
            rft[pl.ds(at, BLK), :] = xbuf[u].astype(bf16).T + mrow[pl.ds(k, 1), :].astype(bf16)
            colacc[pl.ds(at, BLK), :] = jnp.full((BLK, BLK), 4 * BIG, f32)
        return c

    lax.fori_loop(0, NR // UN // 2, prepare, 0)

    def along_y(start, size):
        for k in (4, 3, 5, 2, 6, 1, 7):
            pltpu.make_async_remote_copy(
                src_ref=rows.at[pl.ds(start, size)], dst_ref=red_y.at[y, pl.ds(start, size)],
                send_sem=y_send, recv_sem=y_recv,
                device_id=at_y(k), device_id_type=MESH,
            ).start()

    def compute(i_step, group):
        for i in range(NX):
            slot = group * NX + i
            hot = (iota((K - SEND, BLK), 0) == slot).astype(f32).astype(bf16)
            gop[0:SEND, i * BLK:(i + 1) * BLK] = gbuf[slot]
            gop[SEND:K, i * BLK:(i + 1) * BLK] = hot
        d = jnp.dot(rft[...], gop[...], preferred_element_type=f32)
        acc = jnp.min(d.reshape(NR * BLK // 8, 8, NX * BLK), axis=0)
        m = jnp.minimum(
            jnp.minimum(d[:, 0:BLK], d[:, BLK:2 * BLK]),
            jnp.minimum(d[:, 2 * BLK:3 * BLK], d[:, 3 * BLK:4 * BLK]),
        )
        colacc[...] = jnp.minimum(colacc[...], m)
        low = jnp.min(acc, axis=0, keepdims=True)
        for i in range(NX):
            rows[i_step * NX + i] = low[:, i * BLK:(i + 1) * BLK]

    def own_arrived(u):
        for a in range(2):

            @pl.when(source(x, u, a) != b)
            def _():
                first(u, a).wait_recv()

    def ring(way, u, step, behind):
        sign = 1 - 2 * way
        group = 2 * lax.rem(x - sign * (step - behind) + NX, NX) + u
        if step == 2:
            piece = gbuf.at[pl.ds(group * NX + way * (NX // 2), NX // 2)]
        else:
            piece = gbuf.at[pl.ds(group * NX, NX)]
        return pltpu.make_async_remote_copy(
            src_ref=piece, dst_ref=piece,
            send_sem=ring_send.at[way, u, step - 1], recv_sem=ring_recv.at[way, u, step - 1],
            device_id=at_x(sign + NX), device_id_type=MESH,
        )

    def leave(u):
        own_arrived(u)
        for way in range(2):
            ring(way, u, 1, 1).start()

    def pass_on(u):
        for way in range(2):
            ring(way, u, 1, 0).wait_recv()
            ring(way, u, 2, 1).start()

    def last_arrived(u):
        for way in range(2):
            ring(way, u, 2, 0).wait_recv()

    leave(0)
    lax.fori_loop(NR // UN // 2, NR // UN, prepare, 0)

    def group_step(i, c):
        for at, what, u in (
            (1, leave, 1), (2, pass_on, 0), (4, pass_on, 1), (6, last_arrived, 0), (7, last_arrived, 1)
        ):

            @pl.when(i == at)
            def _():
                what(u)

        near = (i > 1) & (i < 6)
        u = jnp.where(near, (i - 2) // 2, lax.rem(i, 2))
        away = jnp.where(near, 3 - 2 * lax.rem(i, 2), jnp.where(i < 2, 0, 2))
        compute(i, 2 * lax.rem(x + away, NX) + u)

        @pl.when(i == 5)
        def _():
            along_y(0, 6 * NX)

        @pl.when(i == 7)
        def _():
            along_y(6 * NX, 2 * NX)

        return c

    lax.fori_loop(0, NY, group_step, 0)

    def finish(first_k, c):
        for u in range(UN):
            k = first_k * UN + u
            at = pl.multiple_of(k * BLK, BLK)
            v = colacc[pl.ds(at, BLK), :].T
            rd_ref[pl.ds(k, 1), :] = jnp.min(v, axis=0, keepdims=True) / F
        return c

    lax.fori_loop(0, NR // UN // 2, finish, 0)

    pltpu.make_async_copy(red_y.at[pl.ds(0, NY - 1)], red_y.at[pl.ds(0, NY - 1)], y_recv).wait()
    for i in range(2 * NX):
        at = i * NX
        low = rows[at:at + NX]
        for k in range(1, NY):
            low = jnp.minimum(low, red_y[lax.rem(y + k, NY), at:at + NX])
        u, away = ((i - 2) // 2, 3 - 2 * (i % 2)) if 1 < i < 6 else (i % 2, 0 if i < 2 else 2)
        for j in range(NX):
            fin[2 * source(lax.rem(x + away, NX), u, j // 2) + j % 2] = low[j]

    pl.semaphore_wait(known, NX - 1)

    def deliver(j, c):
        off = far_first(j, NB)
        s = lax.rem(b + off, NB)
        for k in (2, 1, 3, 0):

            @pl.when((off != 0) | (k != 0))
            def _():
                pltpu.make_async_remote_copy(
                    src_ref=fin.at[pl.ds(2 * s, 2)], dst_ref=back.at[x, pl.ds(2 * b, 2)],
                    send_sem=z_send, recv_sem=z_recv,
                    device_id=(s, lax.rem(x + k, NX) * NY + y), device_id_type=MESH,
                ).start()

        return c

    lax.fori_loop(0, NB, deliver, 0)
    back[x, pl.ds(2 * b, 2)] = fin[pl.ds(2 * b, 2)]
    lax.fori_loop(NR // UN // 2, NR // UN, finish, 0)
    pltpu.make_async_copy(sized, sized, z_recv).wait()

    for i in range(NR):
        low = jnp.minimum(jnp.minimum(back[0, i], back[1, i]), jnp.minimum(back[2, i], back[3, i]))
        back2[i:i + 1, :] = low / F
    hi, mid, lo = three(back2[...])
    parts = jnp.concatenate([hi, mid, lo], axis=0).astype(bf16)
    for q in range(0, Q, 4):
        cols = slice(q * BLK, (q + 4) * BLK)
        v = jnp.dot(parts, onehot[:, cols], preferred_element_type=f32)
        v = v[0:NR] + v[NR:2 * NR] + v[2 * NR:3 * NR]
        pick = iota((NR, 4 * BLK), 0) == blk_row[:, cols]
        v = jnp.sum(jnp.where(pick, v, 0.0), axis=0, keepdims=True)
        for i in range(4):
            gd_ref[q + i:q + i + 1, :] = v[:, i * BLK:(i + 1) * BLK]

    for u in range(2):
        for a in range(2):

            @pl.when(target(u, a) != b)
            def _():
                first(u, a).wait_send()

        for way in range(2):
            for step in (1, 2):
                ring(way, u, step, 1).wait_send()
    pltpu.make_async_copy(red_y.at[0:NY - 1], red_y.at[0:NY - 1], y_send).wait()
    pltpu.make_async_copy(sized, sized, z_send).wait()


def per_device(gen_points, bucket_id, ref_points, block_pairs, pair_count):
    vmem = pl.BlockSpec(memory_space=pltpu.VMEM)
    dma = pltpu.SemaphoreType.DMA
    gd, rd = pl.pallas_call(
        kernel,
        out_shape=(
            jax.ShapeDtypeStruct((Q, BLK), f32),
            jax.ShapeDtypeStruct((NR, BLK), f32),
        ),
        in_specs=[pl.BlockSpec(memory_space=pltpu.HBM)] * 4 + [pl.BlockSpec(memory_space=pltpu.SMEM)],
        out_specs=(vmem, vmem),
        scratch_shapes=[
            pltpu.VMEM((F, GEN), bf16),
            pltpu.VMEM((Q, BLK), jnp.int32),
            pltpu.VMEM((F, NR, BLK), bf16),
            pltpu.VMEM((1, 1, 2, PAIRS), jnp.int32),
            dma((4,)),
            pltpu.VMEM((NX, SEND, GEN), bf16),
            pltpu.VMEM((F * NR, BLK), f32),
            pltpu.VMEM((3, NR, BLK), f32),
            pltpu.VMEM((BLK, GEN), bf16),
            pltpu.VMEM((1, GEN), f32),
            pltpu.VMEM((1, GEN), jnp.int32),
            pltpu.VMEM((Q * NB, BLK), bf16),
            pltpu.VMEM((NX, SEND, BLK), f32),
            pltpu.VMEM((UN, K, BLK), f32),
            pltpu.VMEM((NR, K), f32),
            pltpu.VMEM((NR * BLK, K), bf16),
            pltpu.VMEM((2, 2, 2, SEND, BLK), bf16),
            pltpu.VMEM((NR, SEND, BLK), bf16),
            pltpu.VMEM((K, NX * BLK), bf16),
            pltpu.VMEM((NR * BLK, BLK), f32),
            pltpu.VMEM((NR, 1, BLK), f32),
            pltpu.VMEM((NY, NR, 1, BLK), f32),
            pltpu.VMEM((NR, 1, BLK), f32),
            pltpu.VMEM((NX, NR, 1, BLK), f32),
            pltpu.VMEM((NX * NR - 2, 1, BLK), f32),
            pltpu.VMEM((NR, BLK), f32),
            dma((2, 2)), dma((2, 2)), dma((2, 2, 2)), dma((2, 2, 2)),
            dma, dma, dma, dma, pltpu.SemaphoreType.REGULAR,
        ],
        compiler_params=pltpu.CompilerParams(
            collective_id=0, has_side_effects=True, vmem_limit_bytes=56 * 2**20
        ),
        cost_estimate=pl.CostEstimate(
            flops=2 * 4096 * 4096 * 128, bytes_accessed=2**21, transcendentals=0
        ),
        name="chamfer",
    )(
        gen_points, bucket_id.reshape(Q, BLK), ref_points.transpose(1, 0, 2), block_pairs,
        pair_count,
    )
    return gd.reshape(GEN), rd


def solution(mesh):
    return jax.shard_map(
        per_device,
        mesh=mesh,
        in_specs=(
            P(None, "bucket"),
            P("bucket"),
            P(("bucket", "ref"), None, None),
            P("bucket", "ref", None, None),
            P("bucket", "ref"),
        ),
        out_specs=(P("bucket"), P(("bucket", "ref"), None)),
        check_vma=False,
    )
```

```python
import jax
import jax.numpy as jnp
from jax import lax
from jax.experimental import pallas as pl
from jax.experimental.pallas import tpu as pltpu
from jax.sharding import PartitionSpec as P

F = 68
BLK = 128
NB = 16
NR = 32
NX = 4
NY = 8
GEN = 3072
Q = GEN // BLK
PAIRS = 768
SEND = 80
K = 128
UN = 8
BIG = 1e30
MESH = pl.DeviceIdType.MESH
bf16 = jnp.bfloat16
f32 = jnp.float32


def iota(shape, dim):
    return lax.broadcasted_iota(jnp.int32, shape, dim)


def three(v):
    hi = v.astype(bf16).astype(f32)
    mid = (v - hi).astype(bf16).astype(f32)
    lo = (v - hi - mid).astype(bf16).astype(f32)
    return hi, mid, lo


def kernel(
    gen_hbm, bid_hbm, rp_hbm, pairs_hbm, count_ref,
    gd_ref, rd_ref,
    gen_ref, bid_ref, rp_ref, pairs_ref, in_sem, picked,
    rpf, rnorm,
    onehot, rank_row, blk_row, ebuf, tmp, xbuf, mrow, rft, gsend, gbuf, gop, colacc,
    rows, red_y, fin, back, sized, back2,
    s1_send, s1_recv, ring_send, ring_recv, y_send, y_recv, z_send, z_recv, known,
):
    b = lax.axis_index("bucket")
    r = lax.axis_index("ref")
    x, y = r // NY, lax.rem(r, NY)
    def quarter(k, c):
        return 4 * lax.rem(b // 4 + k, 4) + c

    def source(at_x, u, a):
        c = lax.rem(at_x - b + NB, 4)
        k = jnp.where(c // 2 - lax.rem(b, 4) // 2 == 1, 3, 1)
        return quarter(2 * u if a == 0 else (4 - k if u else k), c)

    def target(u, a):
        c = lax.rem(x - b + NB, 4)
        k = jnp.where(c // 2 - lax.rem(b, 4) // 2 == -1, 1, 3)
        return quarter(2 * u if a == 0 else (4 - k if u else k), c)

    bar = pltpu.get_barrier_semaphore()

    def at_x(i):
        return (b, lax.rem(x + i, NX) * NY + y)

    def at_y(i):
        return (b, x * NY + lax.rem(y + i, NY))

    def at_z(i):
        return (lax.rem(b + i, NB), r)

    def far_first(j, count):
        return count // 2 + (j // 2) * (1 - lax.rem(j, 2)) - (j // 2 + 1) * lax.rem(j, 2)

    for peer, count in ((at_z, NB), (at_y, NY), (at_x, NX)):
        def greet(j, c, peer=peer, count=count):
            to = peer(far_first(j, count))
            pl.semaphore_signal(bar, inc=1, device_id=to, device_id_type=MESH)
            return c

        lax.fori_loop(0, count - 1, greet, 0)

    loads = [
        pltpu.make_async_copy(src, dst, in_sem.at[i])
        for i, (src, dst) in enumerate(
            [(bid_hbm, bid_ref), (gen_hbm, gen_ref), (pairs_hbm, pairs_ref), (rp_hbm, rp_ref)]
        )
    ]
    for copy in loads:
        copy.start()

    loads[0].wait()
    for q in range(Q):
        ebuf[q * NB:(q + 1) * NB, :] = (bid_ref[q:q + 1, :] == iota((NB, BLK), 0)).astype(f32).astype(bf16)
    i0, i1 = iota((BLK, 2 * BLK), 0), iota((BLK, 2 * BLK), 1)
    tri = ((i0 < i1) | (i1 >= BLK)).astype(f32).astype(bf16)
    sums = jnp.dot(ebuf[...], tri, preferred_element_type=f32)
    carry = jnp.zeros((NB, BLK), f32)
    for q in range(Q):
        e = ebuf[q * NB:(q + 1) * NB, :].astype(f32)
        part = sums[q * NB:(q + 1) * NB, :]
        rank = jnp.sum(e * (part[:, :BLK] + carry), axis=0, keepdims=True)
        carry = carry + part[:, BLK:]
        over = rank >= BLK
        off = jnp.where(over, rank - BLK, rank)
        rank_row[:, q * BLK:(q + 1) * BLK] = off
        blk = 2 * bid_ref[q:q + 1, :] + over.astype(jnp.int32)
        blk_row[:, q * BLK:(q + 1) * BLK] = blk
        onehot[:, q * BLK:(q + 1) * BLK] = (iota((BLK, BLK), 0) == off.astype(jnp.int32)).astype(f32).astype(bf16)

    def first(u, a):
        return pltpu.make_async_remote_copy(
            src_ref=gsend.at[u, a], dst_ref=gbuf.at[pl.ds((2 * x + u) * NX + 2 * a, 2)],
            send_sem=s1_send.at[u, a], recv_sem=s1_recv.at[u, a],
            device_id=(target(u, a), r), device_id_type=MESH,
        )

    loads[1].wait()
    for i in range(NX):
        picked[i, F:SEND, :] = jnp.zeros((SEND - F, GEN), bf16)
    for u in range(2):
        for i in range(NX):
            mine = (blk_row[...] == 2 * target(u, i // 2) + i % 2).astype(f32).astype(bf16)
            picked[i, 0:F, :] = gen_ref[...] * mine
        blocks = lax.dot_general(
            picked[...].reshape(NX * SEND, GEN), onehot[...], (((1,), (1,)), ((), ())),
            preferred_element_type=f32,
        )
        for i in range(NX):
            block = blocks[i * SEND:(i + 1) * SEND]
            norm = jnp.sum(block * block, axis=0, keepdims=True)
            total = jnp.sum(
                jnp.where(iota((NB, BLK), 0) == target(u, i // 2), carry, 0.0), axis=0, keepdims=True
            )
            slot_id = iota((1, BLK), 1) + (i % 2) * BLK
            norm = jnp.where(slot_id.astype(f32) < total, norm, BIG)
            tmp[i] = block
            for j, part in enumerate(three(norm)):
                tmp[i, F + j:F + j + 1, :] = part
            tmp[i, F + 3:F + 6, :] = jnp.ones((3, BLK), f32)
            gsend[u, i // 2, i % 2] = tmp[i].astype(bf16)

        if u == 0:
            pl.semaphore_wait(bar, NB + NX + NY - 3)
            for k in range(1, NX):
                pl.semaphore_signal(known, inc=1, device_id=at_x(k), device_id_type=MESH)

        for a in range(2):

            @pl.when(target(u, a) != b)
            def _():
                first(u, a).start()

            @pl.when(target(u, a) == b)
            def _():
                gbuf[pl.ds((2 * x + u) * NX + 2 * a, 2)] = gsend[u, a]

    loads[2].wait()
    kid = iota((K, PAIRS), 0) - SEND
    c = ((kid >> 3) - b + NB) & 3
    k = jnp.where((c >> 1) - lax.rem(b, 4) // 2 == 1, 3, 1)
    far = ((kid >> 2) & 1) == 1
    k = jnp.where((kid & 2) == 0, jnp.where(far, 2, 0), jnp.where(far, 4 - k, k))
    gid = 8 * ((b // 4 + k) & 3) + 2 * c + (kid & 1)
    gid = jnp.where((kid >= 0) & (kid < NR), gid, -1)
    live = iota((1, PAIRS), 1) < count_ref[0, 0]
    named = jnp.where(live, pairs_ref[0, 0, 0:1, :], -2)
    a_hot = (gid == named).astype(f32).astype(bf16)
    b_hot = (iota((NR, PAIRS), 0) == pairs_ref[0, 0, 1:2, :]).astype(f32).astype(bf16)
    listed = lax.dot_general(b_hot, a_hot, (((1,), (1,)), ((), ())), preferred_element_type=f32)
    lane = iota((NR, K), 1)
    mrow[...] = jnp.where(
        (lane >= SEND) & (lane < SEND + NR) & (listed < 0.5), BIG,
        jnp.where((lane >= F) & (lane < F + 3), 1.0, 0.0),
    )

    loads[3].wait()
    v = rp_ref[...].astype(f32)
    for i, part in enumerate(three(jnp.sum(v * v, axis=0))):
        rnorm[i] = part
    rpf[...] = (-2.0 * v).reshape(F * NR, BLK)
    for u in range(UN):
        xbuf[u, F:K, :] = jnp.zeros((K - F, BLK), f32)

    def prepare(first_k, c):
        for u in range(UN):
            k = first_k * UN + u
            xbuf[u, 0:F, :] = rpf[pl.ds(k, F, stride=NR), :]
            for i in range(3):
                xbuf[u, F + 3 + i:F + 4 + i, :] = rnorm[i, pl.ds(k, 1), :]
        for u in range(UN):
            k = first_k * UN + u
            at = pl.multiple_of(k * BLK, BLK)
            rft[pl.ds(at, BLK), :] = xbuf[u].astype(bf16).T + mrow[pl.ds(k, 1), :].astype(bf16)
            colacc[pl.ds(at, BLK), :] = jnp.full((BLK, BLK), 4 * BIG, f32)
        return c

    lax.fori_loop(0, NR // UN // 2, prepare, 0)

    def along_y(part, start, size):
        for k in (4, 3, 5, 2, 6, 1, 7):
            pltpu.make_async_remote_copy(
                src_ref=rows.at[pl.ds(start, size)], dst_ref=red_y.at[y, pl.ds(start, size)],
                send_sem=y_send, recv_sem=y_recv.at[part],
                device_id=at_y(k), device_id_type=MESH,
            ).start()

    def compute(i_step, group):
        for i in range(NX):
            slot = group * NX + i
            hot = (iota((K - SEND, BLK), 0) == slot).astype(f32).astype(bf16)
            gop[0:SEND, i * BLK:(i + 1) * BLK] = gbuf[slot]
            gop[SEND:K, i * BLK:(i + 1) * BLK] = hot
        d = jnp.dot(rft[...], gop[...], preferred_element_type=f32)
        acc = jnp.min(d.reshape(NR * BLK // 8, 8, NX * BLK), axis=0)
        m = jnp.minimum(
            jnp.minimum(d[:, 0:BLK], d[:, BLK:2 * BLK]),
            jnp.minimum(d[:, 2 * BLK:3 * BLK], d[:, 3 * BLK:4 * BLK]),
        )
        colacc[...] = jnp.minimum(colacc[...], m)
        low = jnp.min(acc, axis=0, keepdims=True)
        for i in range(NX):
            rows[i_step * NX + i] = low[:, i * BLK:(i + 1) * BLK]

    def own_arrived(u):
        for a in range(2):

            @pl.when(source(x, u, a) != b)
            def _():
                first(u, a).wait_recv()

    def ring(way, u, step, behind):
        sign = 1 - 2 * way
        group = 2 * lax.rem(x - sign * (step - behind) + NX, NX) + u
        if step == 2:
            piece = gbuf.at[pl.ds(group * NX + way * (NX // 2), NX // 2)]
        else:
            piece = gbuf.at[pl.ds(group * NX, NX)]
        return pltpu.make_async_remote_copy(
            src_ref=piece, dst_ref=piece,
            send_sem=ring_send.at[way, u, step - 1], recv_sem=ring_recv.at[way, u, step - 1],
            device_id=at_x(sign + NX), device_id_type=MESH,
        )

    def leave(u):
        own_arrived(u)
        for way in range(2):
            ring(way, u, 1, 1).start()

    def pass_on(u):
        for way in range(2):
            ring(way, u, 1, 0).wait_recv()
            ring(way, u, 2, 1).start()

    def last_arrived(u):
        for way in range(2):
            ring(way, u, 2, 0).wait_recv()

    leave(0)
    lax.fori_loop(NR // UN // 2, NR // UN, prepare, 0)

    def group_step(i, c):
        for at, what, u in (
            (1, leave, 1), (2, pass_on, 0), (4, pass_on, 1), (6, last_arrived, 0), (7, last_arrived, 1)
        ):

            @pl.when(i == at)
            def _():
                what(u)

        near = (i > 1) & (i < 6)
        u = jnp.where(near, (i - 2) // 2, lax.rem(i, 2))
        away = jnp.where(near, 3 - 2 * lax.rem(i, 2), jnp.where(i < 2, 0, 2))
        compute(i, 2 * lax.rem(x + away, NX) + u)

        @pl.when(i == 5)
        def _():
            along_y(0, 0, 6 * NX)

        @pl.when(i == 7)
        def _():
            along_y(1, 6 * NX, 2 * NX)

        return c

    lax.fori_loop(0, NY, group_step, 0)

    def finish(first_k, c):
        for u in range(UN):
            k = first_k * UN + u
            at = pl.multiple_of(k * BLK, BLK)
            v = colacc[pl.ds(at, BLK), :].T
            rd_ref[pl.ds(k, 1), :] = jnp.min(v, axis=0, keepdims=True) / F
        return c

    def reduce_y(part, groups):
        size = len(groups) * NX
        whole = red_y.at[0:NY - 1, 0:size]
        pltpu.make_async_copy(whole, whole, y_recv.at[part]).wait()
        for i in groups:
            at = i * NX
            low = rows[at:at + NX]
            for k in range(1, NY):
                low = jnp.minimum(low, red_y[lax.rem(y + k, NY), at:at + NX])
            u, away = ((i - 2) // 2, 3 - 2 * (i % 2)) if 1 < i < 6 else (i % 2, 0 if i < 2 else 2)
            for j in range(NX):
                fin[2 * source(lax.rem(x + away, NX), u, j // 2) + j % 2] = low[j]

    def deliver(aways):
        for k in (2, 1, 3, 0):
            for u in (1, 0):
                for a in range(2):
                    for away in aways:
                        s = source(lax.rem(x + away, NX), u, a)

                        @pl.when((s != b) | (k != 0))
                        def _():
                            pltpu.make_async_remote_copy(
                                src_ref=fin.at[pl.ds(2 * s, 2)], dst_ref=back.at[x, pl.ds(2 * b, 2)],
                                send_sem=z_send, recv_sem=z_recv,
                                device_id=(s, lax.rem(x + k, NX) * NY + y), device_id_type=MESH,
                            ).start()

    pl.semaphore_wait(known, NX - 1)
    reduce_y(0, range(6))
    deliver((0, 3, 1))
    lax.fori_loop(0, NR // UN // 4, finish, 0)
    reduce_y(1, (6, 7))
    deliver((2,))
    back[x, pl.ds(2 * b, 2)] = fin[pl.ds(2 * b, 2)]
    lax.fori_loop(NR // UN // 4, NR // UN, finish, 0)
    pltpu.make_async_copy(sized, sized, z_recv).wait()

    for i in range(NR):
        low = jnp.minimum(jnp.minimum(back[0, i], back[1, i]), jnp.minimum(back[2, i], back[3, i]))
        back2[i:i + 1, :] = low / F
    hi, mid, lo = three(back2[...])
    parts = jnp.concatenate([hi, mid, lo], axis=0).astype(bf16)
    for q in range(0, Q, 4):
        cols = slice(q * BLK, (q + 4) * BLK)
        v = jnp.dot(parts, onehot[:, cols], preferred_element_type=f32)
        v = v[0:NR] + v[NR:2 * NR] + v[2 * NR:3 * NR]
        pick = iota((NR, 4 * BLK), 0) == blk_row[:, cols]
        v = jnp.sum(jnp.where(pick, v, 0.0), axis=0, keepdims=True)
        for i in range(4):
            gd_ref[q + i:q + i + 1, :] = v[:, i * BLK:(i + 1) * BLK]

    for u in range(2):
        for a in range(2):

            @pl.when(target(u, a) != b)
            def _():
                first(u, a).wait_send()

        for way in range(2):
            for step in (1, 2):
                ring(way, u, step, 1).wait_send()
    pltpu.make_async_copy(red_y.at[0:NY - 1], red_y.at[0:NY - 1], y_send).wait()
    pltpu.make_async_copy(sized, sized, z_send).wait()


def per_device(gen_points, bucket_id, ref_points, block_pairs, pair_count):
    vmem = pl.BlockSpec(memory_space=pltpu.VMEM)
    dma = pltpu.SemaphoreType.DMA
    gd, rd = pl.pallas_call(
        kernel,
        out_shape=(
            jax.ShapeDtypeStruct((Q, BLK), f32),
            jax.ShapeDtypeStruct((NR, BLK), f32),
        ),
        in_specs=[pl.BlockSpec(memory_space=pltpu.HBM)] * 4 + [pl.BlockSpec(memory_space=pltpu.SMEM)],
        out_specs=(vmem, vmem),
        scratch_shapes=[
            pltpu.VMEM((F, GEN), bf16),
            pltpu.VMEM((Q, BLK), jnp.int32),
            pltpu.VMEM((F, NR, BLK), bf16),
            pltpu.VMEM((1, 1, 2, PAIRS), jnp.int32),
            dma((4,)),
            pltpu.VMEM((NX, SEND, GEN), bf16),
            pltpu.VMEM((F * NR, BLK), f32),
            pltpu.VMEM((3, NR, BLK), f32),
            pltpu.VMEM((BLK, GEN), bf16),
            pltpu.VMEM((1, GEN), f32),
            pltpu.VMEM((1, GEN), jnp.int32),
            pltpu.VMEM((Q * NB, BLK), bf16),
            pltpu.VMEM((NX, SEND, BLK), f32),
            pltpu.VMEM((UN, K, BLK), f32),
            pltpu.VMEM((NR, K), f32),
            pltpu.VMEM((NR * BLK, K), bf16),
            pltpu.VMEM((2, 2, 2, SEND, BLK), bf16),
            pltpu.VMEM((NR, SEND, BLK), bf16),
            pltpu.VMEM((K, NX * BLK), bf16),
            pltpu.VMEM((NR * BLK, BLK), f32),
            pltpu.VMEM((NR, 1, BLK), f32),
            pltpu.VMEM((NY, NR, 1, BLK), f32),
            pltpu.VMEM((NR, 1, BLK), f32),
            pltpu.VMEM((NX, NR, 1, BLK), f32),
            pltpu.VMEM((NX * NR - 2, 1, BLK), f32),
            pltpu.VMEM((NR, BLK), f32),
            dma((2, 2)), dma((2, 2)), dma((2, 2, 2)), dma((2, 2, 2)),
            dma, dma((2,)), dma, dma, pltpu.SemaphoreType.REGULAR,
        ],
        compiler_params=pltpu.CompilerParams(
            collective_id=0, has_side_effects=True, vmem_limit_bytes=56 * 2**20
        ),
        cost_estimate=pl.CostEstimate(
            flops=2 * 4096 * 4096 * 128, bytes_accessed=2**21, transcendentals=0
        ),
        name="chamfer",
    )(
        gen_points, bucket_id.reshape(Q, BLK), ref_points.transpose(1, 0, 2), block_pairs,
        pair_count,
    )
    return gd.reshape(GEN), rd


def solution(mesh):
    return jax.shard_map(
        per_device,
        mesh=mesh,
        in_specs=(
            P(None, "bucket"),
            P("bucket"),
            P(("bucket", "ref"), None, None),
            P("bucket", "ref", None, None),
            P("bucket", "ref"),
        ),
        out_specs=(P("bucket"), P(("bucket", "ref"), None)),
        check_vma=False,
    )
```
